256 devices in a mesh: row: 8 (over x, core), col: 32 (over y, z).
Axes of the slice: x: 4, y: 4, z: 8, core: 2. Of those that a mesh axis runs over, the one named last changes fastest.
Arguments:
- src_points: bfloat16 [64, 32768], P(None, ('row', 'col')), may hold values from -6 to 6
- tgt_points: bfloat16 [64, 32768], P(None, ('col', 'row')), may hold values from -6 to 6
- src_dual: float32 [32768], P('row'), may hold values from 0.8 to 1.2
- tgt_dual: float32 [32768], P('col'), may hold values from 0.8 to 1.2
- src_cot: float32 [32768], P('row'), may hold values from -2.5 to 6.5
- tgt_cot: float32 [32768], P('col'), may hold values from -2.5 to 6.5
Outputs:
- src_grad: float32 [64, 32768], P(None, ('row', 'col'))
- tgt_grad: float32 [64, 32768], P(None, ('col', 'row'))
The draws below stay inside these ranges and needn't reach their ends.
All inputs are finite; a program needn't handle non-finite values.
Results may differ from the reference program's by a relative error of at most 0.00045.
Values may be sent and summed in bfloat16 or wider, within the bound.
No kernel may reach another device: no remote copies, remote signals or barrier semaphores. Data moves between devices by JAX's collectives and lax.ppermute only.
A program may use at most 64 MiB of HBM per device.

```python
import jax
import jax.numpy as jnp
from jax import lax

D = 64
NS = 32768
NT = 32768


def cot_values(key, count, start, stop):
    place = jnp.arange(count, dtype=jnp.float32) / float(max(count - 1, 1))
    offset = start + (stop - start) * place
    noise = jnp.clip(jax.random.normal(key, (count,), jnp.float32), -3.5, 3.5)
    return (offset + noise).astype(jnp.float32)


def draw_src_cot(key, part):
    key = jax.random.fold_in(key, 11)
    return cot_values(key, NS, 1.0, 3.0)


def draw_tgt_cot(key, part):
    key = jax.random.fold_in(key, 23)
    return cot_values(key, NT, 1.0, 3.0)


def levels(stream_key, extent, split, low, top_value):
    def one(dim, blocks):
        steps = jax.random.uniform(jax.random.fold_in(jax.random.fold_in(stream_key, 6), dim), (blocks,), jnp.float32, low / len(split), top_value / len(split))
        return jnp.repeat(jnp.exp(steps), extent[dim] // blocks).reshape((-1,) + (1,) * (len(extent) - dim - 1))

    factor_of = one(*split[0])
    for cut in split[1:]:
        factor_of = factor_of * one(*cut)
    return factor_of


def bell_draw(key, shape, spread, bound, cuts=(), kind=jnp.bfloat16):
    loudness = levels(key, shape, cuts, -0.22, 0.18) if cuts else 1.0
    values = jax.random.normal(key, shape, jnp.float32) * spread * loudness
    return jnp.minimum(jnp.maximum(values, -bound), bound).astype(kind)


def setup_inputs(seed: int = 0) -> dict:
    splits = jax.random.split(jax.random.key(seed), 7)
    src_points = bell_draw(splits[0], (D, NS), 1.0, 6.0, ((1, 256),))
    tgt_points = bell_draw(splits[1], (D, NT), 1.0, 6.0, ((1, 256),))
    src_dual = jnp.clip(0.8 + 0.40000004 * jax.random.uniform(splits[2], (NS,), jnp.float32) ** levels(splits[2], (NS,), ((0, 8),), -0.2, 0.2), 0.8, 1.2)
    tgt_dual = jnp.clip(0.8 + 0.40000004 * jax.random.uniform(splits[3], (NT,), jnp.float32) ** levels(splits[3], (NT,), ((0, 32),), -0.2, 0.2), 0.8, 1.2)
    src_cot = draw_src_cot(jax.random.fold_in(splits[6], 71), 0)
    tgt_cot = draw_tgt_cot(jax.random.fold_in(splits[6], 71), 0)
    return {"src_points": src_points, "tgt_points": tgt_points, "src_dual": src_dual, "tgt_dual": tgt_dual, "src_cot": src_cot, "tgt_cot": tgt_cot}


blur_scale = 0.25
ridge_shift = 0.5

def reference(src_points, tgt_points, src_dual, tgt_dual, src_cot, tgt_cot):
    width = src_points.shape[0]
    src_wide = src_points.astype(jnp.float32)
    tgt_wide = tgt_points.astype(jnp.float32)
    src_norm = lax.optimization_barrier(jnp.sum(src_wide * src_wide, axis=0))
    tgt_norm = lax.optimization_barrier(jnp.sum(tgt_wide * tgt_wide, axis=0))
    step_rows = min(1024, NS)
    blocks = NS // step_rows
    src_tiles = src_points.reshape(width, blocks, step_rows).transpose(1, 0, 2)
    wide_tiles = src_wide.reshape(width, blocks, step_rows).transpose(1, 0, 2)
    norm_tiles = src_norm.reshape(blocks, step_rows)
    dual_tiles = src_dual.reshape(blocks, step_rows)

    def plan_tile(piece, norms, duals):
        dots = lax.dot_general(piece, tgt_points, (((0,), (0,)), ((), ())), preferred_element_type=jnp.float32)
        cost = (norms[:, None] + tgt_norm[None, :] - 2.0 * dots) / width
        return jnp.exp((duals[:, None] + tgt_dual[None, :] - cost) / blur_scale) / NT

    def sweep(row_vec, col_vec):
        vec_tiles = row_vec.reshape(blocks, step_rows)

        def visit(carry, inputs):
            piece, norms, duals, weights = inputs
            plan = plan_tile(piece, norms, duals)
            mass_c = carry[0] + lax.optimization_barrier(jnp.sum(plan, axis=0))
            pulled = carry[1] + lax.optimization_barrier(jnp.sum(plan * weights[:, None], axis=0))
            return ((mass_c, pulled), (lax.optimization_barrier(jnp.sum(plan, axis=1)), lax.optimization_barrier(jnp.sum(plan * col_vec[None, :], axis=1))))
        zero = jnp.zeros((NT,), jnp.float32)
        (mass_c, pulled), (mass_r, pushed) = lax.scan(visit, (zero, zero), (src_tiles, norm_tiles, dual_tiles, vec_tiles))
        return (mass_r.reshape(NS), pushed.reshape(NS), mass_c, pulled)

    def inner(a, b, c, d):
        return jnp.sum(a * b) + jnp.sum(c * d)
    mass_r, pushed, mass_c, pulled = sweep(src_cot, tgt_cot)
    row_mass = mass_r + ridge_shift
    col_mass = mass_c + ridge_shift
    row_image = row_mass * src_cot + pushed
    col_image = col_mass * tgt_cot + pulled
    start_norm = inner(src_cot, src_cot, tgt_cot, tgt_cot)
    alpha = start_norm / inner(src_cot, row_image, tgt_cot, col_image)
    row_sol = alpha * src_cot
    col_sol = alpha * tgt_cot
    row_res = src_cot - alpha * row_image
    col_res = tgt_cot - alpha * col_image
    next_norm = inner(row_res, row_res, col_res, col_res)
    ratio = next_norm / start_norm
    row_dir = row_res + ratio * src_cot
    col_dir = col_res + ratio * tgt_cot
    unused_r, pushed, unused_c, pulled = sweep(row_dir, col_dir)
    row_image = row_mass * row_dir + pushed
    col_image = col_mass * col_dir + pulled
    alpha = next_norm / inner(row_dir, row_image, col_dir, col_image)
    row_sol = row_sol + alpha * row_dir
    col_sol = col_sol + alpha * col_dir
    scale = 2.0 / (blur_scale * width)
    sol_tiles = row_sol.reshape(blocks, step_rows)

    def visit_grad(carry, inputs):
        piece, wide, norms, duals, weights = inputs
        plan = plan_tile(piece, norms, duals)
        mixed = plan * (weights[:, None] + col_sol[None, :])
        toward = lax.dot_general(tgt_wide, mixed, (((1,), (1,)), ((), ())), precision=lax.Precision.HIGHEST)
        row_grad = wide * lax.optimization_barrier(jnp.sum(mixed, axis=1))[None, :] - toward
        back = jnp.dot(wide, mixed, precision=lax.Precision.HIGHEST)
        col_grad = tgt_wide * lax.optimization_barrier(jnp.sum(mixed, axis=0))[None, :] - back
        return (carry + scale * col_grad, scale * row_grad)
    col_total, row_out = lax.scan(visit_grad, jnp.zeros((width, NT), jnp.float32), (src_tiles, wide_tiles, norm_tiles, dual_tiles, sol_tiles))
    src_grad = row_out.transpose(1, 0, 2).reshape(width, NS)
    return (src_grad, col_total)
```

```python
import jax
import jax.numpy as jnp
import numpy as np
from jax import lax
from jax.experimental import pallas as pl
from jax.experimental.pallas import tpu as pltpu
from jax.sharding import Mesh, PartitionSpec as P

blur_scale = 0.25
ridge_shift = 0.5
D = 64
L = 128
KP = 80
SA = ("x", "y")
TA = ("c", "z")
NA = 16
NB = 16
ROWS = NA * L
COLS = NB * L
STEP = 4
BLK = STEP * L
MA = 208
PR = 144
LOG2E = 1.4426950408889634
GAIN = 2.0 * LOG2E / (blur_scale * D)
SHIFT = 15.0 / GAIN
f32 = jnp.float32
bf16 = jnp.bfloat16
HI = lax.Precision.HIGHEST
VMEM = 56 * 1024 * 1024


def split3(v):
    hi = v.astype(bf16)
    rest = v - hi.astype(f32)
    mid = rest.astype(bf16)
    low = (rest - mid.astype(f32)).astype(bf16)
    return hi, mid, low


def join3(block, at):
    return (
        block[at : at + 1].astype(f32)
        + block[at + 1 : at + 2].astype(f32)
        + block[at + 2 : at + 3].astype(f32)
    )


def call(kernel, out_shape, **kw):
    return pl.pallas_call(
        kernel,
        out_shape=out_shape,
        compiler_params=pltpu.CompilerParams(vmem_limit_bytes=VMEM),
        **kw,
    )


def sds(shape, dtype):
    return jax.ShapeDtypeStruct(shape, dtype)


def pack_kernel(src_ref, tgt_ref, sd_ref, td_ref, sc_ref, tc_ref, out_s, out_t):
    si = lax.axis_index("y") * 8 + lax.axis_index("z")
    ti = lax.axis_index("x") * 2 + lax.axis_index("c")
    one = jnp.ones((3, L), bf16)

    def fill(points, dual, cot, first, shift, out):
        wide = points.astype(f32)
        norm = jnp.sum(wide * wide, axis=0, keepdims=True)
        bias = (D / 2.0) * dual - 0.5 * norm - shift
        biases = jnp.concatenate(split3(bias), axis=0)
        cots = jnp.concatenate(split3(cot), axis=0)
        none = jnp.zeros((3, L), bf16)
        pad = jnp.zeros((4, L), bf16)
        if first:
            tail = [biases, one, cots, none, pad]
        else:
            tail = [one, biases, none, cots, pad]
        tail = jnp.concatenate([t.astype(f32) for t in tail], axis=0).astype(bf16)
        whole = jnp.concatenate([points, tail], axis=0)
        out[...] = jnp.broadcast_to(whole[None], out.shape)

    fill(src_ref[...], sd_ref[pl.ds(si, 1), :], sc_ref[pl.ds(si, 1), :], True, SHIFT, out_s)
    fill(tgt_ref[...], td_ref[pl.ds(ti, 1), :], tc_ref[pl.ds(ti, 1), :], False, 0.0, out_t)


def cot_of(block, first):
    return join3(block, 70 if first else 73)


def sweep_kernel(xg, yg, plan, wu_out, wv_out, ya, bv, wu, col, tot):
    step = pl.program_id(0)

    @pl.when(step == 0)
    def _():
        for k in range(NB):
            block = yg[k]
            ya[:, k * L : (k + 1) * L] = block
            bv[:, k * L : (k + 1) * L] = jnp.broadcast_to(cot_of(block, False), (8, L))
        col[...] = jnp.zeros_like(col)
        tot[...] = jnp.zeros_like(tot)

    row_id = lax.broadcasted_iota(jnp.int32, (KP, L), 0)
    pick = jnp.where((row_id >= 70) & (row_id < 73), 1.0, 0.0).astype(bf16)
    ones = jnp.ones((8, L), f32)
    wide = 512
    for s in range(STEP):
        xa = xg[s]
        bu = lax.dot_general(xa, pick, (((0,), (0,)), ((), ())), preferred_element_type=f32)
        bu3 = bu.reshape(16, 8, L)
        acc = jnp.zeros((16, 8, L), f32)
        for n in range(COLS // wide):
            dots = lax.dot_general(
                xa, ya[:, n * wide : (n + 1) * wide], (((0,), (0,)), ((), ())), preferred_element_type=f32
            )
            p = jnp.exp2(dots * GAIN)
            plan[s * L : (s + 1) * L, n * wide : (n + 1) * wide] = p.astype(bf16)
            for m in range(wide // L):
                lo = n * wide + m * L
                pm = p[:, m * L : (m + 1) * L].reshape(16, 8, L)
                mixed = pm * (bu3 + bv[:, lo : lo + L][None])
                acc = acc + mixed
                col[:, lo : lo + L] += jnp.sum(mixed, axis=0)
        part = lax.dot_general(
            ones, acc.reshape(L, L), (((1,), (1,)), ((), ())), precision=HI, preferred_element_type=f32
        )
        wu[pl.ds(step * STEP + s, 1), :] = part[:1]
        own = cot_of(xa, True)
        tot[0:8] += jnp.sum(acc * bu3, axis=0)
        tot[8:9] += own * own

    @pl.when(step == pl.num_programs(0) - 1)
    def _():
        wv = jnp.concatenate(
            [jnp.sum(col[:, k * L : (k + 1) * L], axis=0, keepdims=True) for k in range(NB)], axis=0
        )
        cv = jnp.concatenate([bv[0:1, k * L : (k + 1) * L] for k in range(NB)], axis=0)
        bw = jnp.sum(tot[0:8]) + jnp.sum(wv * cv)
        bb = jnp.sum(tot[8:9]) / NA + jnp.sum(cv * cv) / NB
        mark = lax.broadcasted_iota(jnp.int32, (8, L), 0)
        head = jnp.concatenate([wu[...], jnp.where(mark == 0, bw, bb)], axis=0)
        wu_out[...] = jnp.broadcast_to(head[None], wu_out.shape)
        tail = jnp.concatenate([wv, jnp.zeros((8, L), f32)], axis=0)
        wv_out[...] = jnp.broadcast_to(tail[None], wv_out.shape)


def relay_kernel(got, send_in, send):
    del send_in
    total = got[0]
    for k in range(1, got.shape[0]):
        total = total + got[k]
    send[...] = jnp.broadcast_to(total[None], send.shape)


def grad_kernel(
    plan, xg, yg, wu_in, wv_in, pay_s, pay_t, sum_s, sum_t, scal, ay, ru, rv, bu_all, left, acc_s
):
    step = pl.program_id(0)
    last = pl.num_programs(0) - 1

    @pl.when(step == 0)
    def _():
        wu = wu_in[0]
        wv = wv_in[0]
        for k in range(1, NA):
            wu = wu + wu_in[k]
        for k in range(1, NB):
            wv = wv + wv_in[k]
        bw = wv[16:17]
        bb = wv[17:18]
        alpha = bb / (bw + ridge_shift * bb)
        si = lax.axis_index("x") * 4 + lax.axis_index("y")
        ti = lax.axis_index("c") * 8 + lax.axis_index("z")
        scal[0:1, :] = alpha
        scal[1:2, :] = bb
        scal[2:8, :] = jnp.zeros((6, L), f32)
        ru[...] = wu[0:16]
        rv[...] = wv[0:16]
        sum_s[...] = jnp.broadcast_to(ru[pl.ds(si, 1), :], sum_s.shape)
        sum_t[...] = jnp.broadcast_to(rv[pl.ds(ti, 1), :], sum_t.shape)
        for k in range(NA):
            c = cot_of(xg[k], True)
            bu_all[k : k + 1, :] = c
            ru[k : k + 1, :] = c - alpha * (ru[k : k + 1, :] + ridge_shift * c)
        for k in range(NB):
            c = cot_of(yg[k], False)
            r = c - alpha * (rv[k : k + 1, :] + ridge_shift * c)
            rv[k : k + 1, :] = r
            ay[:, k * L : (k + 1) * L] = stack_side(yg[k], c, r)
        left[...] = jnp.zeros_like(left)
        acc_s[...] = jnp.zeros_like(acc_s)

    p = plan[...]
    lhs = []
    for s in range(STEP):
        at = step * STEP + s
        lhs.append(stack_side(xg[at], bu_all[pl.ds(at, 1), :], ru[pl.ds(at, 1), :]))
    ax = jnp.concatenate(lhs, axis=1)
    left[...] += jnp.dot(ax, p, preferred_element_type=f32)
    right = lax.dot_general(ay[...], p, (((1,), (1,)), ((), ())), preferred_element_type=f32)
    for s in range(STEP):
        at = step * STEP + s
        piece = right[:, s * L : (s + 1) * L]
        block, quad = finish_side(piece, bu_all[pl.ds(at, 1), :], ru[pl.ds(at, 1), :])
        pay_s[pl.ds(at, 1)] = block[None]
        acc_s[0:1, :] += quad

    @pl.when(step == last)
    def _():
        total = acc_s[0:1, :]
        square = jnp.zeros((1, L), f32)
        for k in range(NB):
            r = rv[k : k + 1, :]
            c = cot_of(yg[k], False)
            piece = left[:, k * L : (k + 1) * L]
            block, quad = finish_side(piece, c, r)
            pay_t[k] = block
            total = total + quad
            square = square + r * r / NB + ru[k : k + 1, :] * ru[k : k + 1, :] / NA
        quad = jnp.full((1, L), jnp.sum(total), f32)
        rr = jnp.full((1, L), jnp.sum(square), f32)
        extra = jnp.concatenate([t.astype(f32) for t in split3(quad) + split3(rr)], axis=0)
        for k in range(NA):
            tail = pay_s[k, 128:144, :].astype(f32)
            tail = jnp.concatenate([tail[0:3], extra, tail[9:16]], axis=0)
            pay_s[k, 128:144, :] = tail.astype(bf16)


def stack_side(block, c, r):
    pts = block[0:D]
    wide = pts.astype(f32)
    hi, mid, low = split3(r)
    tail = jnp.concatenate(
        [jnp.ones((1, L), f32), hi.astype(f32), mid.astype(f32), low.astype(f32), jnp.zeros((12, L), f32)],
        axis=0,
    )
    return jnp.concatenate([pts, (wide * c).astype(bf16), (wide * r).astype(bf16), tail.astype(bf16)], axis=0)


def finish_side(piece, c, r):
    base = piece[0:D]
    mass = piece[192:193]
    pushed = piece[193:194] + piece[194:195] + piece[195:196]
    t_b = c * base + piece[D : 2 * D]
    t_r = r * base + piece[2 * D : 3 * D]
    s_r = r * mass + pushed
    hi, mid, low = split3(s_r)
    tail = jnp.concatenate([hi.astype(f32), mid.astype(f32), low.astype(f32), jnp.zeros((13, L), f32)], axis=0)
    block = jnp.concatenate([t_b, t_r, tail], axis=0).astype(bf16)
    return block, r * s_r


def merge_kernel(got, send_in, total_out, send):
    total = got[0].astype(f32)
    for k in range(1, NA):
        total = total + got[k].astype(f32)
    total_out[...] = total
    quad = join3(total, 131)
    rr = join3(total, 134)
    extra = jnp.concatenate([t.astype(f32) for t in split3(quad) + split3(rr)], axis=0)
    for k in range(NB):
        tail = send_in[k].astype(f32)
        send[k] = jnp.concatenate([tail[0:3], extra, tail[9:16]], axis=0).astype(bf16)


def final_kernel(sum_src, got, src_ref, tgt_ref, sum_s, sum_t, scal, out_s, out_t):
    tot_t = got[0].astype(f32)
    for k in range(1, NB):
        tot_t = tot_t + got[k].astype(f32)
    tot_s = sum_src[...]
    alpha = scal[0:1, :]
    bb = scal[1:2, :]
    rr = join3(tot_t, 134)
    quad = join3(tot_t, 131) + ridge_shift * rr
    ratio = rr / bb
    step = rr / (quad - ratio * rr / alpha)
    scale = 2.0 / (blur_scale * D)
    c_b = scale * (alpha + step * ratio)
    c_r = scale * step

    def combine(points, tot, s_b, out):
        s = c_b * s_b + c_r * join3(tot, 128)
        out[...] = points.astype(f32) * s - (c_b * tot[0:D] + c_r * tot[D : 2 * D])

    combine(src_ref[...], tot_s, sum_s[0:1, :], out_s)
    combine(tgt_ref[...], tot_t, sum_t[0:1, :], out_t)


def exchange(v, axes):
    return lax.all_to_all(v, axes, 0, 0, tiled=True)


def body(src_points, tgt_points, src_dual, tgt_dual, src_cot, tgt_cot):
    pay_s, pay_t = call(pack_kernel, (sds((NA, KP, L), bf16), sds((NB, KP, L), bf16)))(
        src_points,
        tgt_points,
        src_dual.reshape(-1, L),
        tgt_dual.reshape(-1, L),
        src_cot.reshape(-1, L),
        tgt_cot.reshape(-1, L),
    )
    xg = exchange(pay_s, SA)
    yg = exchange(pay_t, TA)
    steps = NA // STEP
    full = lambda *shape: pl.BlockSpec(shape, lambda i: (0,) * len(shape))
    plan, wu, wv = call(
        sweep_kernel,
        (sds((ROWS, COLS), bf16), sds((NA, 24, L), f32), sds((NB, 24, L), f32)),
        grid=(steps,),
        in_specs=[pl.BlockSpec((STEP, KP, L), lambda i: (i, 0, 0)), full(NB, KP, L)],
        out_specs=(pl.BlockSpec((BLK, COLS), lambda i: (i, 0)), full(NA, 24, L), full(NB, 24, L)),
        scratch_shapes=[
            pltpu.VMEM((KP, COLS), bf16),
            pltpu.VMEM((8, COLS), f32),
            pltpu.VMEM((NA, L), f32),
            pltpu.VMEM((8, COLS), f32),
            pltpu.VMEM((16, L), f32),
        ],
    )(xg, yg)
    wu = exchange(wu, SA)
    tail = lambda n, rows, at: pl.BlockSpec((n, rows, L), lambda i: (0, at, 0))
    wv = call(
        relay_kernel,
        sds((NB, 24, L), f32),
        grid=(1,),
        in_specs=[tail(NA, 8, 2), tail(NB, 8, 2)],
        out_specs=tail(NB, 8, 2),
        input_output_aliases={1: 0},
    )(wu, wv)
    wv = exchange(wv, TA)
    pay_s, pay_t, sum_s, sum_t, scal = call(
        grad_kernel,
        (
            sds((NA, PR, L), bf16),
            sds((NB, PR, L), bf16),
            sds((8, L), f32),
            sds((8, L), f32),
            sds((8, L), f32),
        ),
        grid=(steps,),
        in_specs=[
            pl.BlockSpec((BLK, COLS), lambda i: (i, 0)),
            full(NA, KP, L),
            full(NB, KP, L),
            full(NA, 24, L),
            full(NB, 24, L),
        ],
        out_specs=(full(NA, PR, L), full(NB, PR, L), full(8, L), full(8, L), full(8, L)),
        scratch_shapes=[
            pltpu.VMEM((MA, COLS), bf16),
            pltpu.VMEM((NA, L), f32),
            pltpu.VMEM((NB, L), f32),
            pltpu.VMEM((NA, L), f32),
            pltpu.VMEM((MA, COLS), f32),
            pltpu.VMEM((8, L), f32),
        ],
    )(plan, xg, yg, wu, wv)
    got_s = exchange(pay_s, SA)
    sum_src, pay_t = call(
        merge_kernel,
        (sds((PR, L), f32), sds((NB, PR, L), bf16)),
        grid=(1,),
        in_specs=[full(NA, PR, L), tail(NB, 16, 8)],
        out_specs=(full(PR, L), tail(NB, 16, 8)),
        input_output_aliases={1: 1},
    )(got_s, pay_t)
    got_t = exchange(pay_t, TA)
    return call(final_kernel, (sds((D, L), f32), sds((D, L), f32)))(
        sum_src, got_t, src_points, tgt_points, sum_s, sum_t, scal
    )


def solution(mesh):
    grid = Mesh(mesh.devices.reshape(4, 2, 4, 8), ("x", "c", "y", "z"))
    in_specs = (
        P(None, ("x", "c", "y", "z")),
        P(None, ("y", "z", "x", "c")),
        P(("x", "c")),
        P(("y", "z")),
        P(("x", "c")),
        P(("y", "z")),
    )
    out_specs = (P(None, ("x", "c", "y", "z")), P(None, ("y", "z", "x", "c")))
    return jax.shard_map(body, mesh=grid, in_specs=in_specs, out_specs=out_specs, check_vma=False)
```

```python
import jax
import jax.numpy as jnp
import numpy as np
from jax import lax
from jax.experimental import pallas as pl
from jax.experimental.pallas import tpu as pltpu
from jax.sharding import Mesh, PartitionSpec as P

blur_scale = 0.25
ridge_shift = 0.5
D = 64
L = 128
KP = 80
SA = ("x", "y")
NA = 16
NB = 16
NZ = 8
ROWS = NA * L
COLS = NB * L
MB = 144
MW = 80
PR = 144
LOG2E = 1.4426950408889634
GAIN = 2.0 * LOG2E / (blur_scale * D)
SHIFT = 15.0 / GAIN
f32 = jnp.float32
bf16 = jnp.bfloat16
HI = lax.Precision.HIGHEST
VMEM = 24 * 1024 * 1024


def split3(v):
    hi = v.astype(bf16)
    rest = v - hi.astype(f32)
    mid = rest.astype(bf16)
    low = (rest - mid.astype(f32)).astype(bf16)
    return hi, mid, low


def join3(block, at):
    return (
        block[at : at + 1].astype(f32)
        + block[at + 1 : at + 2].astype(f32)
        + block[at + 2 : at + 3].astype(f32)
    )


def sds(shape, dtype):
    return jax.ShapeDtypeStruct(shape, dtype)


def call(kernel, out_shape, flops=0, **kw):
    cost = pl.CostEstimate(flops=flops, bytes_accessed=1 << 20, transcendentals=0)
    return pl.pallas_call(
        kernel,
        out_shape=out_shape,
        cost_estimate=cost,
        compiler_params=pltpu.CompilerParams(vmem_limit_bytes=VMEM),
        **kw,
    )


def encode(points, dual, cot, first):
    one = jnp.ones((3, L), f32)
    none = jnp.zeros((3, L), f32)
    wide = points.astype(f32)
    norm = jnp.sum(wide * wide, axis=0, keepdims=True)
    bias = (D / 2.0) * dual - 0.5 * norm
    if first:
        bias = bias - SHIFT
    biases = [t.astype(f32) for t in split3(bias)]
    cots = [t.astype(f32) for t in split3(cot)]
    tail = biases + [one] + cots + [none] if first else [one] + biases + [none] + cots
    tail = jnp.concatenate(tail + [jnp.zeros((4, L), f32)], axis=0).astype(bf16)
    return jnp.concatenate([points, tail], axis=0)


def cot_of(block, first):
    return join3(block, 70 if first else 73)


def encode_src(points, dual, cot, out):
    at = lax.axis_index("y") * 8 + lax.axis_index("z")
    out[...] = encode(points[...], dual[pl.ds(at, 1), :], cot[pl.ds(at, 1), :], True)


def encode_tgt(points, other, dual, cot, out):
    core = lax.axis_index("c")
    at = lax.axis_index("x") * 2
    own = points[...].astype(f32)
    sib = other[...].astype(f32)
    flip = core == 0
    low = jnp.where(flip, own, sib).astype(bf16)
    high = jnp.where(flip, sib, own).astype(bf16)
    both = jnp.concatenate(
        [
            encode(low, dual[pl.ds(at, 1), :], cot[pl.ds(at, 1), :], False),
            encode(high, dual[pl.ds(at + 1, 1), :], cot[pl.ds(at + 1, 1), :], False),
        ],
        axis=0,
    )
    out[...] = jnp.broadcast_to(both[None], out.shape)


def sweep_kernel(g0, g1, g2, g3, yg, plan, xs, cots, wu_out, wv_out, xt, ya, bub, bvb, row, col):
    mx = lax.axis_index("x")
    my = lax.axis_index("y")
    for m, g in enumerate((g0, g1, g2, g3)):
        for k in range(4):
            at = lax.rem(mx + 4 - k, 4) * 4 + lax.rem(my + 4 - m, 4)
            xs[pl.ds(at, 1)] = g[k][None]
    pad = jnp.zeros((L - KP, L), f32)
    row_id = lax.broadcasted_iota(jnp.int32, (L, L), 0)
    pick = jnp.where((row_id >= 70) & (row_id < 73), 1.0, 0.0).astype(bf16)
    for k in range(NA):
        sl = slice(k * L, (k + 1) * L)
        block = xs[k]
        turned = jnp.concatenate([block.astype(f32), pad], axis=0).T.astype(bf16)
        xt[sl, :] = turned
        bub[sl, :] = jnp.dot(turned, pick, preferred_element_type=f32)
        cots[k : k + 1, :] = cot_of(block, True)
        other = yg[k]
        ya[:, sl] = jnp.concatenate([other, pad.astype(bf16)], axis=0)
        c = cot_of(other, False)
        cots[NA + k : NA + k + 1, :] = c
        bvb[:, sl] = jnp.broadcast_to(c, (8, L))
    rb, wide = 512, 256
    for n in range(COLS // wide):
        for r in range(ROWS // rb):
            rows = slice(r * rb, (r + 1) * rb)
            dots = jnp.dot(xt[rows, :], ya[:, n * wide : (n + 1) * wide], preferred_element_type=f32)
            p = jnp.exp2(dots * GAIN)
            plan[rows, n * wide : (n + 1) * wide] = p.astype(bf16)
            bu = bub[rows, :].reshape(rb // 8, 8, L)
            acc = None if n == 0 else row[rows, :].reshape(rb // 8, 8, L)
            for m in range(wide // L):
                sl = slice(n * wide + m * L, n * wide + (m + 1) * L)
                mixed = p[:, m * L : (m + 1) * L].reshape(rb // 8, 8, L) * (bu + bvb[:, sl][None])
                acc = mixed if acc is None else acc + mixed
                down = jnp.sum(mixed, axis=0)
                col[:, sl] = down if r == 0 else col[:, sl] + down
            row[rows, :] = acc.reshape(rb, L)
    wu = jnp.concatenate(
        [jnp.sum(row[k * L : (k + 1) * L, :].T, axis=0, keepdims=True) for k in range(NA)], axis=0
    )
    wv = jnp.concatenate(
        [jnp.sum(col[:, k * L : (k + 1) * L], axis=0, keepdims=True) for k in range(NB)], axis=0
    )
    bu = cots[0:NA]
    bv = cots[NA : NA + NB]
    bw = jnp.sum(wu * bu + wv * bv)
    bb = jnp.sum(bu * bu) / NA + jnp.sum(bv * bv) / NB
    mark = lax.broadcasted_iota(jnp.int32, (8, L), 0)
    head = jnp.concatenate([wu, jnp.where(mark == 0, bw, bb)], axis=0)
    wu_out[...] = jnp.broadcast_to(head[None], wu_out.shape)
    wv_out[...] = wv


def stack_cot(block, c):
    pts = block[0:D]
    tail = [jnp.ones((1, L), f32)] + [t.astype(f32) for t in split3(c)] + [jnp.zeros((12, L), f32)]
    tail = jnp.concatenate(tail, axis=0).astype(bf16)
    return jnp.concatenate([pts, (pts.astype(f32) * c).astype(bf16), tail], axis=0)


def stack_one(block, c):
    tail = [t.astype(f32) for t in split3(c)] + [jnp.zeros((13, L), f32)]
    tail = jnp.concatenate(tail, axis=0).astype(bf16)
    return jnp.concatenate([(block[0:D].astype(f32) * c).astype(bf16), tail], axis=0)


def first_kernel(plan, xs, yg, cots, right, left, ax, ay):
    for k in range(NA):
        ax[:, k * L : (k + 1) * L] = stack_cot(xs[k], cots[k : k + 1, :])
        ay[:, k * L : (k + 1) * L] = stack_cot(yg[k], cots[NA + k : NA + k + 1, :])
    wide = 256
    for r in range(ROWS // wide):
        part = lax.dot_general(
            ay[...], plan[r * wide : (r + 1) * wide, :], (((1,), (1,)), ((), ())), preferred_element_type=f32
        )
        for m in range(2):
            at = 2 * r + m
            right[:, at * L : (at + 1) * L] = fold_cot(part[:, m * L : (m + 1) * L], cots[at : at + 1, :])
    for n in range(COLS // wide):
        part = jnp.dot(ax[...], plan[:, n * wide : (n + 1) * wide], preferred_element_type=f32)
        for m in range(2):
            at = 2 * n + m
            c = cots[NA + at : NA + at + 1, :]
            left[:, at * L : (at + 1) * L] = fold_cot(part[:, m * L : (m + 1) * L], c)


def fold_cot(part, c):
    tail = part[2 * D : 2 * D + 16]
    pushed = tail[1:2] + tail[2:3] + tail[3:4]
    tail = jnp.concatenate([tail[0:1], pushed, jnp.zeros((14, L), f32)], axis=0)
    return jnp.concatenate([part[0:D], c * part[0:D] + part[D : 2 * D], tail], axis=0)


def relay_kernel(got, own, sib, send):
    total = got[0]
    for k in range(1, got.shape[0]):
        total = total + got[k]
    whole = jnp.concatenate([own[...] + sib[...], total], axis=0)
    send[...] = jnp.broadcast_to(whole[None], send.shape)


def second_kernel(plan, yg, cots, wu_in, wv_in, right, out, sums, aw):
    wu = wu_in[0, 0:NA]
    for k in range(1, NA):
        wu = wu + wu_in[k, 0:NA]
    wv = wv_in[0, 0:NB]
    for k in range(1, NZ):
        wv = wv + wv_in[k, 0:NB]
    sums[0:NA] = wu
    sums[NA : NA + NB] = wv
    for k in range(NB):
        w = sums[NA + k : NA + k + 1, :] + ridge_shift * cots[NA + k : NA + k + 1, :]
        aw[:, k * L : (k + 1) * L] = stack_one(yg[k], w)
    wide = 256
    for r in range(ROWS // wide):
        part = lax.dot_general(
            aw[...], plan[r * wide : (r + 1) * wide, :], (((1,), (1,)), ((), ())), preferred_element_type=f32
        )
        for m in range(2):
            at = 2 * r + m
            sl = slice(at * L, (at + 1) * L)
            w = sums[at : at + 1, :] + ridge_shift * cots[at : at + 1, :]
            piece = part[:, m * L : (m + 1) * L]
            pushed = piece[D : D + 1] + piece[D + 1 : D + 2] + piece[D + 2 : D + 3]
            out[0:D, sl] = w * right[0:D, sl] + piece[0:D]
            out[D : D + 8, sl] = jnp.broadcast_to(pushed, (8, L))


def step_of(wv_in, wv_sib):
    total = wv_in[0, NB : NB + 8]
    for k in range(1, NZ):
        total = total + wv_in[k, NB : NB + 8]
    for k in range(NZ):
        total = total + wv_sib[k, NB : NB + 8]
    bw = total[0:1]
    bb = total[1:2]
    return bb / (bw + ridge_shift * bb), bb


def payload_of(t_b, t_r, s_r, rest):
    tail = jnp.concatenate([t.astype(f32) for t in split3(s_r)] + rest, axis=0)
    return jnp.concatenate([t_b, t_r, tail], axis=0).astype(bf16)


def send_kernel(right, second, cots, sums, wv_in, wv_sib, left_tail, pay, scal):
    alpha, bb = step_of(wv_in, wv_sib)
    bu, bv = cots[0:NA], cots[NA : NA + NB]
    ru = bu - alpha * (sums[0:NA] + ridge_shift * bu)
    rv = bv - alpha * (sums[NA : NA + NB] + ridge_shift * bv)
    rr = jnp.sum(ru * ru) / NA + jnp.sum(rv * rv) / NB
    quad = jnp.zeros((1, L), f32)
    s_rows = []
    for k in range(NA):
        sl = slice(k * L, (k + 1) * L)
        r = ru[k : k + 1]
        mass = right[2 * D : 2 * D + 1, sl]
        pushed = right[2 * D + 1 : 2 * D + 2, sl] - alpha * second[D : D + 1, sl]
        s_r = r * mass + pushed
        s_rows.append(s_r)
        quad = quad + r * (s_r + pushed)
        v = rv[k : k + 1]
        quad = quad + v * v * left_tail[0:1, sl]
    quad = jnp.full((1, L), jnp.sum(quad), f32)
    rr = jnp.full((1, L), rr, f32)
    extra = [t.astype(f32) for t in split3(quad) + split3(rr)] + [jnp.zeros((7, L), f32)]
    for k in range(NA):
        sl = slice(k * L, (k + 1) * L)
        t_b = right[D : 2 * D, sl]
        t_r = t_b - alpha * second[0:D, sl]
        pay[k] = payload_of(t_b, t_r, s_rows[k], extra)
    scal[0:1, :] = alpha
    scal[1:2, :] = bb
    scal[2:8, :] = jnp.zeros((6, L), f32)


def third_kernel(plan, xs, cots, sums, left, scal, mine, other, aw):
    core = lax.axis_index("c")
    for k in range(NA):
        w = sums[k : k + 1, :] + ridge_shift * cots[k : k + 1, :]
        aw[:, k * L : (k + 1) * L] = stack_one(xs[k], w)
    alpha = scal[0:1, :]
    none = [jnp.zeros((13, L), f32)]
    wide = 256
    for n in range(COLS // wide):
        part = jnp.dot(aw[...], plan[:, n * wide : (n + 1) * wide], preferred_element_type=f32)
        blocks = []
        for m in range(2):
            at = 2 * n + m
            sl = slice(at * L, (at + 1) * L)
            piece = part[:, m * L : (m + 1) * L]
            c = cots[NA + at : NA + at + 1, :]
            w = sums[NA + at : NA + at + 1, :] + ridge_shift * c
            r = c - alpha * w
            t_b = left[D : 2 * D, sl]
            t_r = t_b - alpha * (w * left[0:D, sl] + piece[0:D])
            pushed = piece[D : D + 1] + piece[D + 1 : D + 2] + piece[D + 2 : D + 3]
            s_r = r * left[2 * D : 2 * D + 1, sl] + left[2 * D + 1 : 2 * D + 2, sl] - alpha * pushed
            blocks.append(payload_of(t_b, t_r, s_r, none))

        @pl.when(core == 0)
        def _():
            mine[n] = blocks[0]
            other[n] = blocks[1]

        @pl.when(core != 0)
        def _():
            mine[n] = blocks[1]
            other[n] = blocks[0]


def join_kernel(mine, got, send):
    a = mine[...].astype(f32)
    b = got[...].astype(f32)
    total = a + b
    send[...] = total.astype(bf16)
    for k in range(NZ):
        s = join3(mine[k], 128) + join3(got[k], 128)
        tail = jnp.concatenate([t.astype(f32) for t in split3(s)] + [jnp.zeros((13, L), f32)], axis=0)
        send[k, 128:144, :] = tail.astype(bf16)


def pass_kernel(got, send_in, send):
    total = got[0].astype(f32)
    for k in range(1, NA):
        total = total + got[k].astype(f32)
    quad = join3(total, 3)
    rr = join3(total, 6)
    extra = jnp.concatenate([t.astype(f32) for t in split3(quad) + split3(rr)], axis=0)
    for k in range(NZ):
        tail = send_in[k].astype(f32)
        send[k] = jnp.concatenate([tail[0:3], extra, tail[9:16]], axis=0).astype(bf16)


def total_kernel(got, out):
    total = got[0].astype(f32)
    for k in range(1, got.shape[0]):
        total = total + got[k].astype(f32)
    out[...] = total


def final_kernel(tot_s, tot_t, sib, src_ref, tgt_ref, sums, scal, out_s, out_t):
    alpha = scal[0:1, :]
    bb = scal[1:2, :]
    more = sib[0].astype(f32)
    for k in range(1, NZ):
        more = more + sib[k].astype(f32)
    rr = join3(tot_t[...], 134) + join3(more, 6)
    quad = join3(tot_t[...], 131) + join3(more, 3) + ridge_shift * rr
    ratio = rr / bb
    step = rr / (quad - ratio * rr / alpha)
    scale = 2.0 / (blur_scale * D)
    c_b = scale * (alpha + step * ratio)
    c_r = scale * step
    si = lax.axis_index("x") * 4 + lax.axis_index("y")
    ti = lax.axis_index("z") * 2 + lax.axis_index("c")

    def combine(points, tot, s_b, out):
        s = c_b * s_b + c_r * join3(tot, 128)
        out[...] = points[...].astype(f32) * s - (c_b * tot[0:D] + c_r * tot[D : 2 * D])

    combine(src_ref, tot_s[...], sums[pl.ds(si, 1), :], out_s)
    combine(tgt_ref, tot_t[...], sums[pl.ds(NA + ti, 1), :], out_t)


def exchange(v, axes):
    return lax.all_to_all(v, axes, 0, 0, tiled=True)


def shift(v, axis, n, k):
    return lax.ppermute(v, axis, [(i, (i + k) % n) for i in range(n)])


def swap(v):
    return shift(v, "c", 2, 1)


def body(src_points, tgt_points, src_dual, tgt_dual, src_cot, tgt_cot):
    whole = lambda v: v.reshape(-1, L)
    own = call(encode_src, sds((KP, L), bf16))(src_points, whole(src_dual), whole(src_cot))
    send = call(encode_tgt, sds((NZ, 2 * KP, L), bf16))(
        tgt_points, swap(tgt_points), whole(tgt_dual), whole(tgt_cot)
    )
    yg = exchange(send, "z").reshape(NB, KP, L)
    g0 = jnp.stack([own] + [shift(own, "x", 4, k) for k in (1, 2, 3)], axis=0)
    g1, g2, g3 = [shift(g0, "y", 4, k) for k in (1, 2, 3)]
    unit = ROWS * COLS * 2
    vm = pltpu.VMEM
    plan, xs, cots, wu, wv = call(
        sweep_kernel,
        (
            sds((ROWS, COLS), bf16),
            sds((NA, KP, L), bf16),
            sds((NA + NB, L), f32),
            sds((NA, 24, L), f32),
            sds((NB, L), f32),
        ),
        flops=unit * 400,
        scratch_shapes=[
            vm((ROWS, L), bf16),
            vm((L, COLS), bf16),
            vm((ROWS, L), f32),
            vm((8, COLS), f32),
            vm((ROWS, L), f32),
            vm((8, COLS), f32),
        ],
    )(g0, g1, g2, g3, yg)
    wu = exchange(wu, SA)
    right, left = call(
        first_kernel,
        (sds((MB, ROWS), f32), sds((MB, COLS), f32)),
        flops=unit * 512,
        scratch_shapes=[vm((MB, ROWS), bf16), vm((MB, COLS), bf16)],
    )(plan, xs, yg, cots)

    def tail(n, rows, at):
        return pl.BlockSpec((n, rows, L), lambda i: (0, at, 0))

    def full(*shape):
        return pl.BlockSpec(shape, lambda i: (0,) * len(shape))

    send = call(
        relay_kernel,
        sds((NZ, 24, L), f32),
        grid=(1,),
        in_specs=[tail(NA, 8, 2), full(NB, L), full(NB, L)],
        out_specs=full(NZ, 24, L),
    )(wu, wv, swap(wv))
    wv = exchange(send, "z")
    wv_sib = swap(wv)
    second, sums = call(
        second_kernel,
        (sds((D + 8, ROWS), f32), sds((NA + NB, L), f32)),
        flops=unit * 256,
        scratch_shapes=[vm((MW, COLS), bf16)],
    )(plan, yg, cots, wu, wv, right)
    pay, scal = call(
        send_kernel,
        (sds((NA, PR, L), bf16), sds((8, L), f32)),
        grid=(1,),
        in_specs=[
            full(MB, ROWS),
            full(D + 8, ROWS),
            full(NA + NB, L),
            full(NA + NB, L),
            full(NZ, 24, L),
            full(NZ, 24, L),
            pl.BlockSpec((8, COLS), lambda i: (2 * D // 8, 0)),
        ],
        out_specs=(full(NA, PR, L), full(8, L)),
    )(right, second, cots, sums, wv, wv_sib, left)
    got_s = exchange(pay, SA)
    mine, other = call(
        third_kernel,
        (sds((NZ, PR, L), bf16), sds((NZ, PR, L), bf16)),
        flops=unit * 256,
        scratch_shapes=[vm((MW, ROWS), bf16)],
    )(plan, xs, cots, sums, left, scal)
    send = call(join_kernel, sds((NZ, PR, L), bf16), flops=unit * 64)(mine, swap(other))
    send = call(
        pass_kernel,
        sds((NZ, PR, L), bf16),
        grid=(1,),
        in_specs=[tail(NA, 16, 8), tail(NZ, 16, 8)],
        out_specs=tail(NZ, 16, 8),
        input_output_aliases={1: 0},
    )(got_s, send)
    got_t = exchange(send, "z")
    tot_s = call(total_kernel, sds((PR, L), f32), flops=unit * 64)(got_s)
    tot_t = call(total_kernel, sds((PR, L), f32), flops=unit * 64)(got_t)
    return call(
        final_kernel,
        (sds((D, L), f32), sds((D, L), f32)),
        grid=(1,),
        in_specs=[
            full(PR, L),
            full(PR, L),
            tail(NZ, 16, 8),
            full(D, L),
            full(D, L),
            full(NA + NB, L),
            full(8, L),
        ],
        out_specs=(full(D, L), full(D, L)),
    )(tot_s, tot_t, swap(got_t), src_points, tgt_points, sums, scal)


def solution(mesh):
    grid = Mesh(mesh.devices.reshape(4, 2, 4, 8), ("x", "c", "y", "z"))
    in_specs = (
        P(None, ("x", "c", "y", "z")),
        P(None, ("y", "z", "x", "c")),
        P(("x", "c")),
        P(("y", "z")),
        P(("x", "c")),
        P(("y", "z")),
    )
    out_specs = (P(None, ("x", "c", "y", "z")), P(None, ("y", "z", "x", "c")))
    return jax.shard_map(body, mesh=grid, in_specs=in_specs, out_specs=out_specs, check_vma=False)
```

```python
import jax
import jax.numpy as jnp
import numpy as np
from jax import lax
from jax.experimental import pallas as pl
from jax.experimental.pallas import tpu as pltpu
from jax.sharding import Mesh, PartitionSpec as P

blur_scale = 0.25
ridge_shift = 0.5
D = 64
L = 128
KP = 80
SA = ("x", "y")
TA = ("c", "z")
NA = 16
NB = 16
NZ = 8
ROWS = NA * L
COLS = NB * L
MB = 144
MW = 80
PR = 144
LOG2E = 1.4426950408889634
GAIN = 2.0 * LOG2E / (blur_scale * D)
SHIFT = 15.0 / GAIN
f32 = jnp.float32
bf16 = jnp.bfloat16
HI = lax.Precision.HIGHEST
VMEM = 24 * 1024 * 1024


def split3(v):
    hi = v.astype(bf16)
    rest = v - hi.astype(f32)
    mid = rest.astype(bf16)
    low = (rest - mid.astype(f32)).astype(bf16)
    return hi, mid, low


def join3(block, at):
    return (
        block[at : at + 1].astype(f32)
        + block[at + 1 : at + 2].astype(f32)
        + block[at + 2 : at + 3].astype(f32)
    )


def sds(shape, dtype):
    return jax.ShapeDtypeStruct(shape, dtype)


def call(kernel, out_shape, flops=0, **kw):
    cost = pl.CostEstimate(flops=flops, bytes_accessed=1 << 20, transcendentals=0)
    return pl.pallas_call(
        kernel,
        out_shape=out_shape,
        cost_estimate=cost,
        compiler_params=pltpu.CompilerParams(vmem_limit_bytes=VMEM),
        **kw,
    )


def encode(points, dual, cot, first):
    one = jnp.ones((3, L), f32)
    none = jnp.zeros((3, L), f32)
    wide = points.astype(f32)
    norm = jnp.sum(wide * wide, axis=0, keepdims=True)
    bias = (D / 2.0) * dual - 0.5 * norm
    if first:
        bias = bias - SHIFT
    biases = [t.astype(f32) for t in split3(bias)]
    cots = [t.astype(f32) for t in split3(cot)]
    tail = biases + [one] + cots + [none] if first else [one] + biases + [none] + cots
    tail = jnp.concatenate(tail + [jnp.zeros((4, L), f32)], axis=0).astype(bf16)
    return jnp.concatenate([points, tail], axis=0)


def cot_of(block, first):
    return join3(block, 70 if first else 73)


def encode_src(points, dual, cot, out):
    at = lax.axis_index("y") * 8 + lax.axis_index("z")
    out[...] = encode(points[...], dual[pl.ds(at, 1), :], cot[pl.ds(at, 1), :], True)


def encode_tgt(points, other, dual, cot, after, out):
    del after
    core = lax.axis_index("c")
    at = lax.axis_index("x") * 2
    own = points[...].astype(f32)
    sib = other[...].astype(f32)
    flip = core == 0
    low = jnp.where(flip, own, sib).astype(bf16)
    high = jnp.where(flip, sib, own).astype(bf16)
    both = jnp.concatenate(
        [
            encode(low, dual[pl.ds(at, 1), :], cot[pl.ds(at, 1), :], False),
            encode(high, dual[pl.ds(at + 1, 1), :], cot[pl.ds(at + 1, 1), :], False),
        ],
        axis=0,
    )
    out[...] = jnp.broadcast_to(both[None], out.shape)


def sweep_kernel(
    g0, g1, g2, g3, yg, plan, xs, cots, wu_out, wv_out, right, left, xt, ya, bub, bvb, row, col, ax, ay
):
    mx = lax.axis_index("x")
    my = lax.axis_index("y")
    for m, g in enumerate((g0, g1, g2, g3)):
        for k in range(4):
            at = lax.rem(mx + 4 - k, 4) * 4 + lax.rem(my + 4 - m, 4)
            xs[pl.ds(at, 1)] = g[k][None]
    pad = jnp.zeros((L - KP, L), f32)
    row_id = lax.broadcasted_iota(jnp.int32, (L, L), 0)
    pick = jnp.where((row_id >= 70) & (row_id < 73), 1.0, 0.0).astype(bf16)
    for k in range(NA):
        sl = slice(k * L, (k + 1) * L)
        block = xs[k]
        ax[:, sl] = stack_cot(block, cot_of(block, True))
        turned = jnp.concatenate([block.astype(f32), pad], axis=0).T.astype(bf16)
        xt[sl, :] = turned
        bub[sl, :] = jnp.dot(turned, pick, preferred_element_type=f32)
        cots[k : k + 1, :] = cot_of(block, True)
        other = yg[k]
        ay[:, sl] = stack_cot(other, cot_of(other, False))
        ya[:, sl] = jnp.concatenate([other, pad.astype(bf16)], axis=0)
        c = cot_of(other, False)
        cots[NA + k : NA + k + 1, :] = c
        bvb[:, sl] = jnp.broadcast_to(c, (8, L))
    rb, wide = 512, 256
    for r in range(ROWS // rb):
        rows = slice(r * rb, (r + 1) * rb)
        bu = bub[rows, :].reshape(rb // 8, 8, L)
        for n in range(COLS // wide):
            dots = jnp.dot(xt[rows, :], ya[:, n * wide : (n + 1) * wide], preferred_element_type=f32)
            p = jnp.exp2(dots * GAIN)
            plan[rows, n * wide : (n + 1) * wide] = p.astype(bf16)
            acc = None if n == 0 else row[rows, :].reshape(rb // 8, 8, L)
            for m in range(wide // L):
                sl = slice(n * wide + m * L, n * wide + (m + 1) * L)
                mixed = p[:, m * L : (m + 1) * L].reshape(rb // 8, 8, L) * (bu + bvb[:, sl][None])
                acc = mixed if acc is None else acc + mixed
                down = jnp.sum(mixed, axis=0)
                col[:, sl] = down if r == 0 else col[:, sl] + down
            row[rows, :] = acc.reshape(rb, L)
        part = lax.dot_general(ay[...], plan[rows, :], (((1,), (1,)), ((), ())), preferred_element_type=f32)
        for m in range(rb // L):
            at = r * (rb // L) + m
            right[:, at * L : (at + 1) * L] = fold_cot(part[:, m * L : (m + 1) * L], cots[at : at + 1, :])
    for n in range(COLS // wide):
        part = jnp.dot(ax[...], plan[:, n * wide : (n + 1) * wide], preferred_element_type=f32)
        for m in range(2):
            at = 2 * n + m
            c = cots[NA + at : NA + at + 1, :]
            left[:, at * L : (at + 1) * L] = fold_cot(part[:, m * L : (m + 1) * L], c)
    wu = jnp.concatenate(
        [jnp.sum(row[k * L : (k + 1) * L, :].T, axis=0, keepdims=True) for k in range(NA)], axis=0
    )
    wv = jnp.concatenate(
        [jnp.sum(col[:, k * L : (k + 1) * L], axis=0, keepdims=True) for k in range(NB)], axis=0
    )
    bu = cots[0:NA]
    bv = cots[NA : NA + NB]
    bw = jnp.sum(wu * bu + wv * bv)
    bb = jnp.sum(bu * bu) / NA + jnp.sum(bv * bv) / NB
    mark = lax.broadcasted_iota(jnp.int32, (8, L), 0)
    head = jnp.concatenate([wu, jnp.where(mark == 0, bw, bb)], axis=0)
    wu_out[...] = jnp.broadcast_to(head[None], wu_out.shape)
    wv_out[...] = wv


def stack_cot(block, c):
    pts = block[0:D]
    tail = [jnp.ones((1, L), f32)] + [t.astype(f32) for t in split3(c)] + [jnp.zeros((12, L), f32)]
    tail = jnp.concatenate(tail, axis=0).astype(bf16)
    return jnp.concatenate([pts, (pts.astype(f32) * c).astype(bf16), tail], axis=0)


def stack_one(block, c):
    tail = [t.astype(f32) for t in split3(c)] + [jnp.zeros((13, L), f32)]
    tail = jnp.concatenate(tail, axis=0).astype(bf16)
    return jnp.concatenate([(block[0:D].astype(f32) * c).astype(bf16), tail], axis=0)


def fold_cot(part, c):
    tail = part[2 * D : 2 * D + 16]
    pushed = tail[1:2] + tail[2:3] + tail[3:4]
    tail = jnp.concatenate([tail[0:1], pushed, jnp.zeros((14, L), f32)], axis=0)
    return jnp.concatenate([part[0:D], c * part[0:D] + part[D : 2 * D], tail], axis=0)


def relay_kernel(got, own, send):
    total = got[0]
    for k in range(1, got.shape[0]):
        total = total + got[k]
    whole = jnp.concatenate([own[...], total], axis=0)
    send[...] = jnp.broadcast_to(whole[None], send.shape)


def payload_of(t_b, t_r, s_r, rest):
    tail = jnp.concatenate([t.astype(f32) for t in split3(s_r)] + rest, axis=0)
    return jnp.concatenate([t_b, t_r, tail], axis=0).astype(bf16)


def left_kernel(plan, xs, cots, wu_in, wv_in, left, right_tail, mine, other, sums, scal, aw):
    wu = wu_in[0, 0:NA]
    for k in range(1, NA):
        wu = wu + wu_in[k, 0:NA]
    wv = wv_in[0]
    for k in range(1, NB):
        wv = wv + wv_in[k]
    bw = wv[NB : NB + 1]
    bb = wv[NB + 1 : NB + 2]
    wv = wv[0:NB]
    alpha = bb / (bw + ridge_shift * bb)
    scal[0:1, :] = alpha
    scal[1:2, :] = bb
    scal[2:8, :] = jnp.zeros((6, L), f32)
    sums[0:NA] = wu
    sums[NA : NA + NB] = wv
    bu, bv = cots[0:NA], cots[NA : NA + NB]
    ru = bu - alpha * (wu + ridge_shift * bu)
    rv = bv - alpha * (wv + ridge_shift * bv)
    rr = jnp.full((1, L), jnp.sum(ru * ru) / NA + jnp.sum(rv * rv) / NB, f32)
    for k in range(NA):
        w = wu[k : k + 1] + ridge_shift * bu[k : k + 1]
        aw[:, k * L : (k + 1) * L] = stack_one(xs[k], w)
    core = lax.axis_index("c")
    quad = jnp.zeros((1, L), f32)
    tails = []
    wide = 256
    for n in range(COLS // wide):
        part = jnp.dot(aw[...], plan[:, n * wide : (n + 1) * wide], preferred_element_type=f32)
        blocks = []
        for m in range(2):
            at = 2 * n + m
            sl = slice(at * L, (at + 1) * L)
            piece = part[:, m * L : (m + 1) * L]
            r = rv[at : at + 1]
            w = wv[at : at + 1] + ridge_shift * bv[at : at + 1]
            t_b = left[D : 2 * D, sl]
            t_r = t_b - alpha * (w * left[0:D, sl] + piece[0:D])
            pushed = piece[D : D + 1] + piece[D + 1 : D + 2] + piece[D + 2 : D + 3]
            pushed = left[2 * D + 1 : 2 * D + 2, sl] - alpha * pushed
            s_r = r * left[2 * D : 2 * D + 1, sl] + pushed
            quad = quad + r * (s_r + pushed)
            u = ru[at : at + 1]
            quad = quad + u * u * right_tail[0:1, sl]
            blocks.append(jnp.concatenate([t_b, t_r], axis=0).astype(bf16))
            tails.append(split3(s_r))

        @pl.when(core == 0)
        def _():
            mine[n, 0 : 2 * D] = blocks[0]
            other[n, 0 : 2 * D] = blocks[1]

        @pl.when(core != 0)
        def _():
            mine[n, 0 : 2 * D] = blocks[1]
            other[n, 0 : 2 * D] = blocks[0]

    quad = jnp.full((1, L), jnp.sum(quad), f32)
    extra = [t.astype(f32) for t in split3(quad) + split3(rr)] + [jnp.zeros((7, L), f32)]
    for n in range(NZ):
        pair = [
            jnp.concatenate([t.astype(f32) for t in tails[2 * n + m]] + extra, axis=0).astype(bf16) for m in range(2)
        ]

        @pl.when(core == 0)
        def _():
            mine[n, 2 * D :] = pair[0]
            other[n, 2 * D :] = pair[1]

        @pl.when(core != 0)
        def _():
            mine[n, 2 * D :] = pair[1]
            other[n, 2 * D :] = pair[0]


def right_kernel(plan, yg, cots, sums, right, out, aw):
    for k in range(NB):
        w = sums[NA + k : NA + k + 1, :] + ridge_shift * cots[NA + k : NA + k + 1, :]
        aw[:, k * L : (k + 1) * L] = stack_one(yg[k], w)
    wide = 256
    for r in range(ROWS // wide):
        part = lax.dot_general(
            aw[...], plan[r * wide : (r + 1) * wide, :], (((1,), (1,)), ((), ())), preferred_element_type=f32
        )
        for m in range(2):
            at = 2 * r + m
            sl = slice(at * L, (at + 1) * L)
            w = sums[at : at + 1, :] + ridge_shift * cots[at : at + 1, :]
            piece = part[:, m * L : (m + 1) * L]
            pushed = piece[D : D + 1] + piece[D + 1 : D + 2] + piece[D + 2 : D + 3]
            out[0:D, sl] = w * right[0:D, sl] + piece[0:D]
            out[D : D + 8, sl] = jnp.broadcast_to(pushed, (8, L))


def send_kernel(right, second, cots, sums, scal, mine, got, pay, send):
    alpha = scal[0:1, :]
    a = mine[0, 2 * D :].astype(f32)
    b = got[0, 2 * D :].astype(f32)
    quad = join3(a, 3) + join3(b, 3)
    rr = join3(a, 6) + join3(b, 6)
    extra = [t.astype(f32) for t in split3(quad) + split3(rr)] + [jnp.zeros((7, L), f32)]
    for k in range(NA):
        sl = slice(k * L, (k + 1) * L)
        c = cots[k : k + 1, :]
        r = c - alpha * (sums[k : k + 1, :] + ridge_shift * c)
        pushed = right[2 * D + 1 : 2 * D + 2, sl] - alpha * second[D : D + 1, sl]
        s_r = r * right[2 * D : 2 * D + 1, sl] + pushed
        t_b = right[D : 2 * D, sl]
        t_r = t_b - alpha * second[0:D, sl]
        pay[k] = payload_of(t_b, t_r, s_r, extra)
    for k in range(NZ):
        t = mine[k, 0 : 2 * D].astype(f32) + got[k, 0 : 2 * D].astype(f32)
        s = join3(mine[k, 2 * D :], 0) + join3(got[k, 2 * D :], 0)
        send[k] = payload_of(t[0:D], t[D:], s, [jnp.zeros((13, L), f32)])


def pass_kernel(got, send_in, tot, send):
    total = got[0].astype(f32)
    for k in range(1, NA):
        total = total + got[k].astype(f32)
    tot[...] = total
    quad = join3(total, 131)
    rr = join3(total, 134)
    extra = [t.astype(f32) for t in split3(quad) + split3(rr)]
    for k in range(NZ):
        tail = send_in[k].astype(f32)
        send[k] = jnp.concatenate([tail[0:3]] + extra + [tail[9:16]], axis=0).astype(bf16)


def final_kernel(tot_s, got, src_ref, tgt_ref, sums, scal, out_s, out_t):
    tot_t = got[0].astype(f32)
    for k in range(1, NZ):
        tot_t = tot_t + got[k].astype(f32)
    alpha = scal[0:1, :]
    bb = scal[1:2, :]
    rr = join3(tot_t, 134)
    quad = join3(tot_t, 131) + ridge_shift * rr
    ratio = rr / bb
    step = rr / (quad - ratio * rr / alpha)
    scale = 2.0 / (blur_scale * D)
    c_b = scale * (alpha + step * ratio)
    c_r = scale * step
    si = lax.axis_index("x") * 4 + lax.axis_index("y")
    ti = lax.axis_index("z") * 2 + lax.axis_index("c")

    def combine(points, tot, s_b, out):
        s = c_b * s_b + c_r * join3(tot, 128)
        out[...] = points[...].astype(f32) * s - (c_b * tot[0:D] + c_r * tot[D : 2 * D])

    combine(src_ref, tot_s[...], sums[pl.ds(si, 1), :], out_s)
    combine(tgt_ref, tot_t, sums[pl.ds(NA + ti, 1), :], out_t)


def exchange(v, axes):
    return lax.all_to_all(v, axes, 0, 0, tiled=True)


def shift(v, axis, n, k):
    return lax.ppermute(v, axis, [(i, (i + k) % n) for i in range(n)])


def swap(v):
    return shift(v, "c", 2, 1)


def body(src_points, tgt_points, src_dual, tgt_dual, src_cot, tgt_cot):
    whole = lambda v: v.reshape(-1, L)
    own = call(encode_src, sds((KP, L), bf16))(src_points, whole(src_dual), whole(src_cot))
    g0 = jnp.stack([own] + [shift(own, "x", 4, k) for k in (1, 2, 3)], axis=0)
    send = call(encode_tgt, sds((NZ, 2 * KP, L), bf16))(
        tgt_points, swap(tgt_points), whole(tgt_dual), whole(tgt_cot), g0
    )
    yg = exchange(send, "z").reshape(NB, KP, L)
    g1, g2, g3 = [shift(g0, "y", 4, k) for k in (1, 2, 3)]
    unit = ROWS * COLS * 2
    vm = pltpu.VMEM
    plan, xs, cots, wu, wv, right, left = call(
        sweep_kernel,
        (
            sds((ROWS, COLS), bf16),
            sds((NA, KP, L), bf16),
            sds((NA + NB, L), f32),
            sds((NA, 24, L), f32),
            sds((NB, L), f32),
            sds((MB, ROWS), f32),
            sds((MB, COLS), f32),
        ),
        flops=unit * 900,
        scratch_shapes=[
            vm((ROWS, L), bf16),
            vm((L, COLS), bf16),
            vm((ROWS, L), f32),
            vm((8, COLS), f32),
            vm((ROWS, L), f32),
            vm((8, COLS), f32),
            vm((MB, ROWS), bf16),
            vm((MB, COLS), bf16),
        ],
    )(g0, g1, g2, g3, yg)
    wu = exchange(wu, SA)

    def tail(n, rows, at):
        return pl.BlockSpec((n, rows, L), lambda i: (0, at, 0))

    def full(*shape):
        return pl.BlockSpec(shape, lambda i: (0,) * len(shape))

    send = call(
        relay_kernel,
        sds((NB, 24, L), f32),
        grid=(1,),
        in_specs=[tail(NA, 8, 2), full(NB, L)],
        out_specs=full(NB, 24, L),
    )(wu, wv)
    wv = exchange(send, TA)
    half = sds((NZ, PR, L), bf16)
    mine, other, sums, scal = call(
        left_kernel,
        (half, half, sds((NA + NB, L), f32), sds((8, L), f32)),
        flops=unit * 256,
        grid=(1,),
        in_specs=[
            full(ROWS, COLS),
            full(NA, KP, L),
            full(NA + NB, L),
            full(NA, 24, L),
            full(NB, 24, L),
            full(MB, COLS),
            pl.BlockSpec((8, ROWS), lambda i: (2 * D // 8, 0)),
        ],
        out_specs=(full(NZ, PR, L), full(NZ, PR, L), full(NA + NB, L), full(8, L)),
        scratch_shapes=[vm((MW, ROWS), bf16)],
    )(plan, xs, cots, wu, wv, left, right)
    got = swap(other)
    second = call(
        right_kernel,
        sds((D + 8, ROWS), f32),
        flops=unit * 256,
        scratch_shapes=[vm((MW, COLS), bf16)],
    )(plan, yg, cots, sums, right)
    pay, send = call(send_kernel, (sds((NA, PR, L), bf16), half))(right, second, cots, sums, scal, mine, got)
    got_s = exchange(pay, SA)
    tot_s, send = call(
        pass_kernel,
        (sds((PR, L), f32), half),
        grid=(1,),
        in_specs=[full(NA, PR, L), tail(NZ, 16, 8)],
        out_specs=(full(PR, L), tail(NZ, 16, 8)),
        input_output_aliases={1: 1},
    )(got_s, send)
    got_t = exchange(send, "z")
    return call(final_kernel, (sds((D, L), f32), sds((D, L), f32)))(
        tot_s, got_t, src_points, tgt_points, sums, scal
    )


def solution(mesh):
    grid = Mesh(mesh.devices.reshape(4, 2, 4, 8), ("x", "c", "y", "z"))
    in_specs = (
        P(None, ("x", "c", "y", "z")),
        P(None, ("y", "z", "x", "c")),
        P(("x", "c")),
        P(("y", "z")),
        P(("x", "c")),
        P(("y", "z")),
    )
    out_specs = (P(None, ("x", "c", "y", "z")), P(None, ("y", "z", "x", "c")))
    return jax.shard_map(body, mesh=grid, in_specs=in_specs, out_specs=out_specs, check_vma=False)
```

```python
import jax
import jax.numpy as jnp
import numpy as np
from jax import lax
from jax.experimental import pallas as pl
from jax.experimental.pallas import tpu as pltpu
from jax.sharding import Mesh, PartitionSpec as P

blur_scale = 0.25
ridge_shift = 0.5
D = 64
L = 128
KP = 80
SA = ("x", "y")
NA = 16
NB = 16
NZ = 8
ROWS = NA * L
COLS = NB * L
MA = 208
PR = 144
LOG2E = 1.4426950408889634
GAIN = 2.0 * LOG2E / (blur_scale * D)
SHIFT = 15.0 / GAIN
f32 = jnp.float32
bf16 = jnp.bfloat16
HI = lax.Precision.HIGHEST
VMEM = 24 * 1024 * 1024
WIDE = 60 * 1024 * 1024


def split3(v):
    hi = v.astype(bf16)
    rest = v - hi.astype(f32)
    mid = rest.astype(bf16)
    low = (rest - mid.astype(f32)).astype(bf16)
    return hi, mid, low


def join3(block, at):
    return (
        block[at : at + 1].astype(f32)
        + block[at + 1 : at + 2].astype(f32)
        + block[at + 2 : at + 3].astype(f32)
    )


def sds(shape, dtype):
    return jax.ShapeDtypeStruct(shape, dtype)


def call(kernel, out_shape, flops=0, limit=VMEM, **kw):
    cost = pl.CostEstimate(flops=flops, bytes_accessed=1 << 20, transcendentals=0)
    return pl.pallas_call(
        kernel,
        out_shape=out_shape,
        cost_estimate=cost,
        compiler_params=pltpu.CompilerParams(vmem_limit_bytes=limit),
        **kw,
    )


def rows16(rows):
    mark = lax.broadcasted_iota(jnp.int32, (16, L), 0)
    out = jnp.zeros((16, L), f32)
    for k, row in enumerate(rows):
        out = jnp.where(mark == k, jnp.broadcast_to(row, (16, L)), out)
    return out


def parts(v):
    return [t.astype(f32) for t in split3(v)]


def encode(points, dual, cot, first):
    one = [jnp.ones((1, L), f32)] * 3
    none = [jnp.zeros((1, L), f32)] * 3
    wide = points.astype(f32)
    norm = jnp.sum(wide * wide, axis=0, keepdims=True)
    bias = (D / 2.0) * dual - 0.5 * norm
    if first:
        bias = bias - SHIFT
    tail = parts(bias) + one + parts(cot) + none if first else one + parts(bias) + none + parts(cot)
    return jnp.concatenate([points, rows16(tail).astype(bf16)], axis=0)


def cot_of(block, first):
    return join3(block, 70 if first else 73)


def encode_kernel(src, tgt, other, src_dual, src_cot, tgt_dual, tgt_cot, own, out):
    at = lax.axis_index("y") * 8 + lax.axis_index("z")
    own[...] = encode(src[...], src_dual[pl.ds(at, 1), :], src_cot[pl.ds(at, 1), :], True)
    at = lax.axis_index("x") * 2
    flip = lax.axis_index("c") == 0
    near = tgt[...].astype(f32)
    far = other[...].astype(f32)
    low = jnp.where(flip, near, far).astype(bf16)
    high = jnp.where(flip, far, near).astype(bf16)
    both = jnp.concatenate(
        [
            encode(low, tgt_dual[pl.ds(at, 1), :], tgt_cot[pl.ds(at, 1), :], False),
            encode(high, tgt_dual[pl.ds(at + 1, 1), :], tgt_cot[pl.ds(at + 1, 1), :], False),
        ],
        axis=0,
    )
    out[...] = jnp.broadcast_to(both[None], out.shape)


def sweep_kernel(g0, g1, g2, g3, yg, plan, xs, cots, wu_out, part_out, xt, ya, bub, bvb, row, col):
    mx = lax.axis_index("x")
    my = lax.axis_index("y")
    for m, g in enumerate((g0, g1, g2, g3)):
        for k in range(4):
            at = lax.rem(mx + 4 - k, 4) * 4 + lax.rem(my + 4 - m, 4)
            xs[pl.ds(at, 1)] = g[k][None]
    pad = jnp.zeros((L - KP, L), f32)
    row_id = lax.broadcasted_iota(jnp.int32, (L, L), 0)
    pick = jnp.where((row_id >= 70) & (row_id < 73), 1.0, 0.0).astype(bf16)
    for k in range(NA):
        sl = slice(k * L, (k + 1) * L)
        block = xs[k]
        turned = jnp.concatenate([block.astype(f32), pad], axis=0).T.astype(bf16)
        xt[sl, :] = turned
        bub[sl, :] = jnp.dot(turned, pick, preferred_element_type=f32)
        cots[k : k + 1, :] = cot_of(block, True)
        other = yg[k]
        ya[:, sl] = jnp.concatenate([other, pad.astype(bf16)], axis=0)
        c = cot_of(other, False)
        cots[NA + k : NA + k + 1, :] = c
        bvb[:, sl] = jnp.broadcast_to(c, (8, L))
    rb, wide = 512, 256
    for r in range(ROWS // rb):
        rows = slice(r * rb, (r + 1) * rb)
        bu = bub[rows, :].reshape(rb // 8, 8, L)
        for n in range(COLS // wide):
            dots = jnp.dot(xt[rows, :], ya[:, n * wide : (n + 1) * wide], preferred_element_type=f32)
            p = jnp.exp2(dots * GAIN)
            plan[rows, n * wide : (n + 1) * wide] = p.astype(bf16)
            acc = None if n == 0 else row[rows, :].reshape(rb // 8, 8, L)
            for m in range(wide // L):
                sl = slice(n * wide + m * L, n * wide + (m + 1) * L)
                mixed = p[:, m * L : (m + 1) * L].reshape(rb // 8, 8, L) * (bu + bvb[:, sl][None])
                acc = mixed if acc is None else acc + mixed
                down = jnp.sum(mixed, axis=0)
                col[:, sl] = down if r == 0 else col[:, sl] + down
            row[rows, :] = acc.reshape(rb, L)
    wu = jnp.concatenate(
        [jnp.sum(row[k * L : (k + 1) * L, :].T, axis=0, keepdims=True) for k in range(NA)], axis=0
    )
    wv = jnp.concatenate(
        [jnp.sum(col[:, k * L : (k + 1) * L], axis=0, keepdims=True) for k in range(NB)], axis=0
    )
    bu = cots[0:NA]
    bv = cots[NA : NA + NB]
    bw = jnp.sum(wu * bu + wv * bv)
    bb = jnp.sum(bu * bu) / NA + jnp.sum(bv * bv) / NB
    mark = lax.broadcasted_iota(jnp.int32, (8, L), 0)
    wu_out[...] = wu
    part_out[...] = jnp.concatenate([wv, jnp.where(mark == 0, bw, bb)], axis=0)


def mix_kernel(wu, parts, send, own):
    total = parts[0] + parts[1]
    own[...] = total[0:NB]
    whole = jnp.concatenate([wu[...], total[NB:]], axis=0)
    send[...] = jnp.broadcast_to(whole[None], send.shape)


def relay_kernel(got, own, send):
    total = got[0]
    for k in range(1, got.shape[0]):
        total = total + got[k]
    whole = jnp.concatenate([own[...], total], axis=0)
    send[...] = jnp.broadcast_to(whole[None], send.shape)


def stack_side(out, sl, block, c, r):
    pts = block[0:D]
    wide = pts.astype(f32)
    out[0:D, sl] = pts
    out[D : 2 * D, sl] = (wide * c).astype(bf16)
    out[2 * D : 3 * D, sl] = (wide * r).astype(bf16)
    out[3 * D : MA, sl] = rows16([jnp.ones((1, L), f32)] + parts(r)).astype(bf16)


def finish_side(piece, c, r):
    base = piece[0:D]
    mass = piece[3 * D : 3 * D + 1]
    pushed = piece[3 * D + 1 : 3 * D + 2] + piece[3 * D + 2 : 3 * D + 3] + piece[3 * D + 3 : 3 * D + 4]
    t_b = c * base + piece[D : 2 * D]
    t_r = r * base + piece[2 * D : 3 * D]
    return t_b, t_r, r * mass + pushed, pushed, mass


def step_kernel(plan, xs, yg, cots, wu_in, wv_in, pay, mine, other, sums, scal, ax, ay):
    wu = wu_in[0, 0:NA]
    for k in range(1, NA):
        wu = wu + wu_in[k, 0:NA]
    wv = wv_in[0]
    for k in range(1, NZ):
        wv = wv + wv_in[k]
    bw = wv[NB : NB + 1]
    bb = wv[NB + 1 : NB + 2]
    wv = wv[0:NB]
    alpha = bb / (bw + ridge_shift * bb)
    scal[0:1, :] = alpha
    scal[1:2, :] = bb
    scal[2:8, :] = jnp.zeros((6, L), f32)
    sums[0:NA] = wu
    sums[NA : NA + NB] = wv
    bu, bv = cots[0:NA], cots[NA : NA + NB]
    ru = bu - alpha * (wu + ridge_shift * bu)
    rv = bv - alpha * (wv + ridge_shift * bv)
    rr = jnp.full((1, L), jnp.sum(ru * ru) / NA + jnp.sum(rv * rv) / NB, f32)
    for k in range(NA):
        stack_side(ax, slice(k * L, (k + 1) * L), xs[k], bu[k : k + 1], ru[k : k + 1])
    for k in range(NB):
        stack_side(ay, slice(k * L, (k + 1) * L), yg[k], bv[k : k + 1], rv[k : k + 1])
    flip = lax.axis_index("c") == 0
    quad = jnp.zeros((1, L), f32)
    tails = []
    wide = 256
    for n in range(COLS // wide):
        part = jnp.dot(ax[...], plan[:, n * wide : (n + 1) * wide], preferred_element_type=f32)
        blocks = []
        for m in range(2):
            at = 2 * n + m
            r = rv[at : at + 1]
            t_b, t_r, s_r, pushed, _ = finish_side(part[:, m * L : (m + 1) * L], bv[at : at + 1], r)
            quad = quad + r * (s_r + pushed)
            blocks.append((t_b, t_r))
            tails.append(s_r)
        (b0, r0), (b1, r1) = blocks
        mine[n, 0:D] = jnp.where(flip, b0, b1).astype(bf16)
        mine[n, D : 2 * D] = jnp.where(flip, r0, r1).astype(bf16)
        other[n, 0:D] = jnp.where(flip, b1, b0).astype(bf16)
        other[n, D : 2 * D] = jnp.where(flip, r1, r0).astype(bf16)
    for n in range(ROWS // wide):
        part = lax.dot_general(
            ay[...], plan[n * wide : (n + 1) * wide, :], (((1,), (1,)), ((), ())), preferred_element_type=f32
        )
        for m in range(2):
            at = 2 * n + m
            r = ru[at : at + 1]
            t_b, t_r, s_r, _, mass = finish_side(part[:, m * L : (m + 1) * L], bu[at : at + 1], r)
            quad = quad + r * r * mass
            pay[at, 0:D] = t_b.astype(bf16)
            pay[at, D : 2 * D] = t_r.astype(bf16)
            pay[at, 2 * D : PR] = rows16(parts(s_r)).astype(bf16)
    quad = jnp.full((1, L), jnp.sum(quad), f32)
    extra = parts(quad) + parts(rr)
    for n in range(NZ):
        s0, s1 = tails[2 * n], tails[2 * n + 1]
        mine[n, 2 * D : PR] = rows16(parts(jnp.where(flip, s0, s1)) + extra).astype(bf16)
        other[n, 2 * D : PR] = rows16(parts(jnp.where(flip, s1, s0)) + extra).astype(bf16)


def join_kernel(mine, both, pay_in, pay, send):
    got = both.at[1 - lax.axis_index("c")]
    a = mine[0, 2 * D :].astype(f32)
    b = got[0, 2 * D :].astype(f32)
    quad = join3(a, 3) + join3(b, 3)
    rr = join3(a, 6) + join3(b, 6)
    mark = lax.broadcasted_iota(jnp.int32, (16, L), 0)
    extra = rows16([jnp.zeros((1, L), f32)] * 3 + parts(quad) + parts(rr))
    for k in range(NA):
        pay[k] = jnp.where(mark < 3, pay_in[k].astype(f32), extra).astype(bf16)
    for k in range(NZ):
        send[k, 0 : 2 * D] = (mine[k, 0 : 2 * D].astype(f32) + got[k, 0 : 2 * D].astype(f32)).astype(bf16)
        s = join3(mine[k, 2 * D :], 0) + join3(got[k, 2 * D :], 0)
        send[k, 2 * D : PR] = rows16(parts(s)).astype(bf16)


def pass_kernel(got, send_in, tot, send):
    total = got[0].astype(f32)
    for k in range(1, NA):
        total = total + got[k].astype(f32)
    tot[...] = total
    quad = join3(total, 131)
    rr = join3(total, 134)
    mark = lax.broadcasted_iota(jnp.int32, (16, L), 0)
    extra = rows16([jnp.zeros((1, L), f32)] * 3 + parts(quad) + parts(rr))
    for k in range(NZ):
        send[k] = jnp.where(mark < 3, send_in[k].astype(f32), extra).astype(bf16)


def final_kernel(tot_s, got, src_ref, tgt_ref, sums, scal, out_s, out_t):
    tot_t = got[0].astype(f32)
    for k in range(1, NZ):
        tot_t = tot_t + got[k].astype(f32)
    alpha = scal[0:1, :]
    bb = scal[1:2, :]
    rr = join3(tot_t, 134)
    quad = join3(tot_t, 131) + ridge_shift * rr
    ratio = rr / bb
    step = rr / (quad - ratio * rr / alpha)
    scale = 2.0 / (blur_scale * D)
    c_b = scale * (alpha + step * ratio)
    c_r = scale * step
    si = lax.axis_index("x") * 4 + lax.axis_index("y")
    ti = lax.axis_index("z") * 2 + lax.axis_index("c")

    def combine(points, tot, s_b, out):
        s = c_b * s_b + c_r * join3(tot, 128)
        out[...] = points[...].astype(f32) * s - (c_b * tot[0:D] + c_r * tot[D : 2 * D])

    combine(src_ref, tot_s[...], sums[pl.ds(si, 1), :], out_s)
    combine(tgt_ref, tot_t, sums[pl.ds(NA + ti, 1), :], out_t)


def exchange(v, axes):
    return lax.all_to_all(v, axes, 0, 0, tiled=True)


def shift(v, axis, n, k):
    return lax.ppermute(v, axis, [(i, (i + k) % n) for i in range(n)])


def swap(v):
    return shift(v, "c", 2, 1)


def pair(v):
    return lax.all_gather(v, "c", axis=0, tiled=False)


def body(src_points, tgt_points, src_dual, tgt_dual, src_cot, tgt_cot):
    whole = lambda v: v.reshape(-1, L)
    own, send = call(encode_kernel, (sds((KP, L), bf16), sds((NZ, 2 * KP, L), bf16)), limit=WIDE)(
        src_points,
        tgt_points,
        swap(tgt_points),
        whole(src_dual),
        whole(src_cot),
        whole(tgt_dual),
        whole(tgt_cot),
    )
    g0 = jnp.stack([own] + [shift(own, "x", 4, k) for k in (1, 2, 3)], axis=0)
    yg = exchange(send, "z").reshape(NB, KP, L)
    g1, g2, g3 = [shift(g0, "y", 4, k) for k in (1, 2, 3)]
    unit = ROWS * COLS * 2
    vm = pltpu.VMEM
    plan, xs, cots, wu, part = call(
        sweep_kernel,
        (
            sds((ROWS, COLS), bf16),
            sds((NA, KP, L), bf16),
            sds((NA + NB, L), f32),
            sds((NA, L), f32),
            sds((NB + 8, L), f32),
        ),
        flops=unit * 400,
        scratch_shapes=[
            vm((ROWS, L), bf16),
            vm((L, COLS), bf16),
            vm((ROWS, L), f32),
            vm((8, COLS), f32),
            vm((ROWS, L), f32),
            vm((8, COLS), f32),
        ],
    )(g0, g1, g2, g3, yg)

    def tail(n, rows, at):
        return pl.BlockSpec((n, rows, L), lambda i: (0, at, 0))

    def full(*shape):
        return pl.BlockSpec(shape, lambda i: (0,) * len(shape))

    send, wv = call(
        mix_kernel,
        (sds((NA, 24, L), f32), sds((NB, L), f32)),
        grid=(1,),
        in_specs=[full(NA, L), full(2, NB + 8, L)],
        out_specs=(full(NA, 24, L), full(NB, L)),
    )(wu, pair(part))
    wu = exchange(send, SA)
    send = call(
        relay_kernel,
        sds((NZ, 24, L), f32),
        grid=(1,),
        in_specs=[tail(NA, 8, 2), full(NB, L)],
        out_specs=full(NZ, 24, L),
    )(wu, wv)
    wv = exchange(send, "z")
    half = sds((NZ, PR, L), bf16)
    pay, mine, other, sums, scal = call(
        step_kernel,
        (sds((NA, PR, L), bf16), half, half, sds((NA + NB, L), f32), sds((8, L), f32)),
        flops=unit * 256,
        scratch_shapes=[vm((MA, ROWS), bf16), vm((MA, COLS), bf16)],
    )(plan, xs, yg, cots, wu, wv)
    pay, send = call(
        join_kernel,
        (sds((NA, PR, L), bf16), half),
        grid=(1,),
        in_specs=[full(NZ, PR, L), full(2, NZ, PR, L), tail(NA, 16, 8)],
        out_specs=(tail(NA, 16, 8), full(NZ, PR, L)),
        input_output_aliases={2: 0},
    )(mine, pair(other), pay)
    got_s = exchange(pay, SA)
    tot_s, send = call(
        pass_kernel,
        (sds((PR, L), f32), half),
        grid=(1,),
        in_specs=[full(NA, PR, L), tail(NZ, 16, 8)],
        out_specs=(full(PR, L), tail(NZ, 16, 8)),
        input_output_aliases={1: 1},
    )(got_s, send)
    got_t = exchange(send, "z")
    return call(final_kernel, (sds((D, L), f32), sds((D, L), f32)))(
        tot_s, got_t, src_points, tgt_points, sums, scal
    )


def solution(mesh):
    grid = Mesh(mesh.devices.reshape(4, 2, 4, 8), ("x", "c", "y", "z"))
    in_specs = (
        P(None, ("x", "c", "y", "z")),
        P(None, ("y", "z", "x", "c")),
        P(("x", "c")),
        P(("y", "z")),
        P(("x", "c")),
        P(("y", "z")),
    )
    out_specs = (P(None, ("x", "c", "y", "z")), P(None, ("y", "z", "x", "c")))
    return jax.shard_map(body, mesh=grid, in_specs=in_specs, out_specs=out_specs, check_vma=False)
```

```python
import jax
import jax.numpy as jnp
import numpy as np
from jax import lax
from jax.experimental import pallas as pl
from jax.experimental.pallas import tpu as pltpu
from jax.sharding import Mesh, PartitionSpec as P

blur_scale = 0.25
ridge_shift = 0.5
D = 64
L = 128
KP = 80
SA = ("x", "y")
NA = 16
NB = 16
NZ = 8
ROWS = NA * L
COLS = NB * L
MA = 208
PR = 144
LOG2E = 1.4426950408889634
GAIN = 2.0 * LOG2E / (blur_scale * D)
SHIFT = 15.0 / GAIN
f32 = jnp.float32
bf16 = jnp.bfloat16
HI = lax.Precision.HIGHEST
VMEM = 24 * 1024 * 1024
WIDE = 60 * 1024 * 1024


def split3(v):
    hi = v.astype(bf16)
    rest = v - hi.astype(f32)
    mid = rest.astype(bf16)
    low = (rest - mid.astype(f32)).astype(bf16)
    return hi, mid, low


def join3(block, at):
    return (
        block[at : at + 1].astype(f32)
        + block[at + 1 : at + 2].astype(f32)
        + block[at + 2 : at + 3].astype(f32)
    )


def sds(shape, dtype):
    return jax.ShapeDtypeStruct(shape, dtype)


def call(kernel, out_shape, flops=0, limit=VMEM, **kw):
    cost = pl.CostEstimate(flops=flops, bytes_accessed=1 << 20, transcendentals=0)
    return pl.pallas_call(
        kernel,
        out_shape=out_shape,
        cost_estimate=cost,
        compiler_params=pltpu.CompilerParams(vmem_limit_bytes=limit),
        **kw,
    )


def rows16(rows):
    mark = lax.broadcasted_iota(jnp.int32, (16, L), 0)
    out = jnp.zeros((16, L), f32)
    for k, row in enumerate(rows):
        out = jnp.where(mark == k, jnp.broadcast_to(row, (16, L)), out)
    return out


def parts(v):
    return [t.astype(f32) for t in split3(v)]


def encode(points, dual, cot, first):
    one = [jnp.ones((1, L), f32)] * 3
    none = [jnp.zeros((1, L), f32)] * 3
    wide = points.astype(f32)
    norm = jnp.sum(wide * wide, axis=0, keepdims=True)
    bias = (D / 2.0) * dual - 0.5 * norm
    if first:
        bias = bias - SHIFT
    tail = parts(bias) + one + parts(cot) + none if first else one + parts(bias) + none + parts(cot)
    return jnp.concatenate([points, rows16(tail).astype(bf16)], axis=0)


def cot_of(block, first):
    return join3(block, 70 if first else 73)


def encode_kernel(src, tgt, other, src_dual, src_cot, tgt_dual, tgt_cot, own, out):
    at = lax.axis_index("y") * 8 + lax.axis_index("z")
    own[...] = encode(src[...], src_dual[pl.ds(at, 1), :], src_cot[pl.ds(at, 1), :], True)
    at = lax.axis_index("x") * 2
    flip = lax.axis_index("c") == 0
    near = tgt[...].astype(f32)
    far = other[...].astype(f32)
    low = jnp.where(flip, near, far).astype(bf16)
    high = jnp.where(flip, far, near).astype(bf16)
    both = jnp.concatenate(
        [
            encode(low, tgt_dual[pl.ds(at, 1), :], tgt_cot[pl.ds(at, 1), :], False),
            encode(high, tgt_dual[pl.ds(at + 1, 1), :], tgt_cot[pl.ds(at + 1, 1), :], False),
        ],
        axis=0,
    )
    out[...] = jnp.broadcast_to(both[None], out.shape)


def stack_kernel(a, b, c, d, out):
    for k, part in enumerate((a, b, c, d)):
        out[k] = part[...]


def sweep_kernel(g0, g1, g2, g3, yg, plan, xs, cots, wu_out, part_out, xt, ya, bub, bvb, row, col):
    mx = lax.axis_index("x")
    my = lax.axis_index("y")
    for m, g in enumerate((g0, g1, g2, g3)):
        for k in range(4):
            at = lax.rem(mx + 4 - k, 4) * 4 + lax.rem(my + 4 - m, 4)
            xs[pl.ds(at, 1)] = g[k][None]
    pad = jnp.zeros((L - KP, L), f32)
    row_id = lax.broadcasted_iota(jnp.int32, (L, L), 0)
    pick = jnp.where((row_id >= 70) & (row_id < 73), 1.0, 0.0).astype(bf16)
    for k in range(NA):
        sl = slice(k * L, (k + 1) * L)
        block = xs[k]
        turned = jnp.concatenate([block.astype(f32), pad], axis=0).T.astype(bf16)
        xt[sl, :] = turned
        bub[sl, :] = jnp.dot(turned, pick, preferred_element_type=f32)
        cots[k : k + 1, :] = cot_of(block, True)
        other = yg[k]
        ya[:, sl] = jnp.concatenate([other, pad.astype(bf16)], axis=0)
        c = cot_of(other, False)
        cots[NA + k : NA + k + 1, :] = c
        bvb[:, sl] = jnp.broadcast_to(c, (8, L))
    rb, wide = 512, 256
    for r in range(ROWS // rb):
        rows = slice(r * rb, (r + 1) * rb)
        bu = bub[rows, :].reshape(rb // 8, 8, L)
        for n in range(COLS // wide):
            dots = jnp.dot(xt[rows, :], ya[:, n * wide : (n + 1) * wide], preferred_element_type=f32)
            p = jnp.exp2(dots * GAIN)
            plan[rows, n * wide : (n + 1) * wide] = p.astype(bf16)
            acc = None if n == 0 else row[rows, :].reshape(rb // 8, 8, L)
            for m in range(wide // L):
                sl = slice(n * wide + m * L, n * wide + (m + 1) * L)
                mixed = p[:, m * L : (m + 1) * L].reshape(rb // 8, 8, L) * (bu + bvb[:, sl][None])
                acc = mixed if acc is None else acc + mixed
                down = jnp.sum(mixed, axis=0)
                col[:, sl] = down if r == 0 else col[:, sl] + down
            row[rows, :] = acc.reshape(rb, L)
    wu = jnp.concatenate(
        [jnp.sum(row[k * L : (k + 1) * L, :].T, axis=0, keepdims=True) for k in range(NA)], axis=0
    )
    wv = jnp.concatenate(
        [jnp.sum(col[:, k * L : (k + 1) * L], axis=0, keepdims=True) for k in range(NB)], axis=0
    )
    bu = cots[0:NA]
    bv = cots[NA : NA + NB]
    bw = jnp.sum(wu * bu + wv * bv)
    bb = jnp.sum(bu * bu) / NA + jnp.sum(bv * bv) / NB
    mark = lax.broadcasted_iota(jnp.int32, (8, L), 0)
    wu_out[...] = wu
    part_out[...] = jnp.concatenate([wv, jnp.where(mark == 0, bw, bb)], axis=0)


def mix_kernel(wu, parts, send, own):
    total = parts[0] + parts[1]
    own[...] = total[0:NB]
    whole = jnp.concatenate([wu[...], total[NB:]], axis=0)
    send[...] = jnp.broadcast_to(whole[None], send.shape)


def relay_kernel(got, own, send):
    total = got[0]
    for k in range(1, got.shape[0]):
        total = total + got[k]
    whole = jnp.concatenate([own[...], total], axis=0)
    send[...] = jnp.broadcast_to(whole[None], send.shape)


def stack_side(out, sl, block, c, r):
    pts = block[0:D]
    wide = pts.astype(f32)
    out[0:D, sl] = pts
    out[D : 2 * D, sl] = (wide * c).astype(bf16)
    out[2 * D : 3 * D, sl] = (wide * r).astype(bf16)
    out[3 * D : MA, sl] = rows16([jnp.ones((1, L), f32)] + parts(r)).astype(bf16)


def finish_side(piece, c, r):
    base = piece[0:D]
    mass = piece[3 * D : 3 * D + 1]
    pushed = piece[3 * D + 1 : 3 * D + 2] + piece[3 * D + 2 : 3 * D + 3] + piece[3 * D + 3 : 3 * D + 4]
    t_b = c * base + piece[D : 2 * D]
    t_r = r * base + piece[2 * D : 3 * D]
    return t_b, t_r, r * mass + pushed, pushed, mass


def step_kernel(plan, xs, yg, cots, wu_in, wv_in, pay, mine, other, sums, scal, ax, ay):
    wu = wu_in[0, 0:NA]
    for k in range(1, NA):
        wu = wu + wu_in[k, 0:NA]
    wv = wv_in[0]
    for k in range(1, NZ):
        wv = wv + wv_in[k]
    bw = wv[NB : NB + 1]
    bb = wv[NB + 1 : NB + 2]
    wv = wv[0:NB]
    alpha = bb / (bw + ridge_shift * bb)
    scal[0:1, :] = alpha
    scal[1:2, :] = bb
    scal[2:8, :] = jnp.zeros((6, L), f32)
    sums[0:NA] = wu
    sums[NA : NA + NB] = wv
    bu, bv = cots[0:NA], cots[NA : NA + NB]
    ru = bu - alpha * (wu + ridge_shift * bu)
    rv = bv - alpha * (wv + ridge_shift * bv)
    rr = jnp.full((1, L), jnp.sum(ru * ru) / NA + jnp.sum(rv * rv) / NB, f32)
    for k in range(NA):
        stack_side(ax, slice(k * L, (k + 1) * L), xs[k], bu[k : k + 1], ru[k : k + 1])
    for k in range(NB):
        stack_side(ay, slice(k * L, (k + 1) * L), yg[k], bv[k : k + 1], rv[k : k + 1])
    flip = lax.axis_index("c") == 0
    quad = jnp.zeros((1, L), f32)
    tails = []
    wide = 256
    for n in range(COLS // wide):
        part = jnp.dot(ax[...], plan[:, n * wide : (n + 1) * wide], preferred_element_type=f32)
        blocks = []
        for m in range(2):
            at = 2 * n + m
            r = rv[at : at + 1]
            t_b, t_r, s_r, pushed, _ = finish_side(part[:, m * L : (m + 1) * L], bv[at : at + 1], r)
            quad = quad + r * (s_r + pushed)
            blocks.append((t_b, t_r))
            tails.append(s_r)
        (b0, r0), (b1, r1) = blocks
        mine[n, 0:D] = jnp.where(flip, b0, b1).astype(bf16)
        mine[n, D : 2 * D] = jnp.where(flip, r0, r1).astype(bf16)
        other[n, 0:D] = jnp.where(flip, b1, b0).astype(bf16)
        other[n, D : 2 * D] = jnp.where(flip, r1, r0).astype(bf16)
    for n in range(ROWS // wide):
        part = lax.dot_general(
            ay[...], plan[n * wide : (n + 1) * wide, :], (((1,), (1,)), ((), ())), preferred_element_type=f32
        )
        for m in range(2):
            at = 2 * n + m
            r = ru[at : at + 1]
            t_b, t_r, s_r, _, mass = finish_side(part[:, m * L : (m + 1) * L], bu[at : at + 1], r)
            quad = quad + r * r * mass
            pay[at, 0:D] = t_b.astype(bf16)
            pay[at, D : 2 * D] = t_r.astype(bf16)
            pay[at, 2 * D : PR] = rows16(parts(s_r)).astype(bf16)
    quad = jnp.full((1, L), jnp.sum(quad), f32)
    extra = parts(quad) + parts(rr)
    for n in range(NZ):
        s0, s1 = tails[2 * n], tails[2 * n + 1]
        mine[n, 2 * D : PR] = rows16(parts(jnp.where(flip, s0, s1)) + extra).astype(bf16)
        other[n, 2 * D : PR] = rows16(parts(jnp.where(flip, s1, s0)) + extra).astype(bf16)


def join_kernel(mine, both, pay_in, pay, send):
    got = both.at[1 - lax.axis_index("c")]
    a = mine[0, 2 * D :].astype(f32)
    b = got[0, 2 * D :].astype(f32)
    quad = join3(a, 3) + join3(b, 3)
    rr = join3(a, 6) + join3(b, 6)
    mark = lax.broadcasted_iota(jnp.int32, (16, L), 0)
    extra = rows16([jnp.zeros((1, L), f32)] * 3 + parts(quad) + parts(rr))
    for k in range(NA):
        pay[k] = jnp.where(mark < 3, pay_in[k].astype(f32), extra).astype(bf16)
    for k in range(NZ):
        send[k, 0 : 2 * D] = (mine[k, 0 : 2 * D].astype(f32) + got[k, 0 : 2 * D].astype(f32)).astype(bf16)
        s = join3(mine[k, 2 * D :], 0) + join3(got[k, 2 * D :], 0)
        send[k, 2 * D : PR] = rows16(parts(s)).astype(bf16)


def pass_kernel(got, send_in, tot, send):
    total = got[0].astype(f32)
    for k in range(1, NA):
        total = total + got[k].astype(f32)
    tot[...] = total
    quad = join3(total, 131)
    rr = join3(total, 134)
    mark = lax.broadcasted_iota(jnp.int32, (16, L), 0)
    extra = rows16([jnp.zeros((1, L), f32)] * 3 + parts(quad) + parts(rr))
    for k in range(NZ):
        send[k] = jnp.where(mark < 3, send_in[k].astype(f32), extra).astype(bf16)


def final_kernel(tot_s, got, src_ref, tgt_ref, sums, scal, out_s, out_t):
    tot_t = got[0].astype(f32)
    for k in range(1, NZ):
        tot_t = tot_t + got[k].astype(f32)
    alpha = scal[0:1, :]
    bb = scal[1:2, :]
    rr = join3(tot_t, 134)
    quad = join3(tot_t, 131) + ridge_shift * rr
    ratio = rr / bb
    step = rr / (quad - ratio * rr / alpha)
    scale = 2.0 / (blur_scale * D)
    c_b = scale * (alpha + step * ratio)
    c_r = scale * step
    si = lax.axis_index("x") * 4 + lax.axis_index("y")
    ti = lax.axis_index("z") * 2 + lax.axis_index("c")

    def combine(points, tot, s_b, out):
        s = c_b * s_b + c_r * join3(tot, 128)
        out[...] = points[...].astype(f32) * s - (c_b * tot[0:D] + c_r * tot[D : 2 * D])

    combine(src_ref, tot_s[...], sums[pl.ds(si, 1), :], out_s)
    combine(tgt_ref, tot_t, sums[pl.ds(NA + ti, 1), :], out_t)


def exchange(v, axes):
    return lax.all_to_all(v, axes, 0, 0, tiled=True)


def shift(v, axis, n, k):
    return lax.ppermute(v, axis, [(i, (i + k) % n) for i in range(n)])


def swap(v):
    return shift(v, "c", 2, 1)


def pair(v):
    return lax.all_gather(v, "c", axis=0, tiled=False)


def body(src_points, tgt_points, src_dual, tgt_dual, src_cot, tgt_cot):
    whole = lambda v: v.reshape(-1, L)
    own, send = call(encode_kernel, (sds((KP, L), bf16), sds((NZ, 2 * KP, L), bf16)), limit=WIDE)(
        src_points,
        tgt_points,
        swap(tgt_points),
        whole(src_dual),
        whole(src_cot),
        whole(tgt_dual),
        whole(tgt_cot),
    )
    g0 = call(stack_kernel, sds((4, KP, L), bf16), flops=10000000000)(
        own, *[shift(own, "x", 4, k) for k in (1, 2, 3)]
    )
    yg = exchange(send, "z").reshape(NB, KP, L)
    g1, g2, g3 = [shift(g0, "y", 4, k) for k in (1, 2, 3)]
    unit = ROWS * COLS * 2
    vm = pltpu.VMEM
    plan, xs, cots, wu, part = call(
        sweep_kernel,
        (
            sds((ROWS, COLS), bf16),
            sds((NA, KP, L), bf16),
            sds((NA + NB, L), f32),
            sds((NA, L), f32),
            sds((NB + 8, L), f32),
        ),
        flops=unit * 400,
        scratch_shapes=[
            vm((ROWS, L), bf16),
            vm((L, COLS), bf16),
            vm((ROWS, L), f32),
            vm((8, COLS), f32),
            vm((ROWS, L), f32),
            vm((8, COLS), f32),
        ],
    )(g0, g1, g2, g3, yg)

    def tail(n, rows, at):
        return pl.BlockSpec((n, rows, L), lambda i: (0, at, 0))

    def full(*shape):
        return pl.BlockSpec(shape, lambda i: (0,) * len(shape))

    send, wv = call(
        mix_kernel,
        (sds((NA, 24, L), f32), sds((NB, L), f32)),
        grid=(1,),
        in_specs=[full(NA, L), full(2, NB + 8, L)],
        out_specs=(full(NA, 24, L), full(NB, L)),
    )(wu, pair(part))
    wu = exchange(send, SA)
    send = call(
        relay_kernel,
        sds((NZ, 24, L), f32),
        grid=(1,),
        in_specs=[tail(NA, 8, 2), full(NB, L)],
        out_specs=full(NZ, 24, L),
    )(wu, wv)
    wv = exchange(send, "z")
    half = sds((NZ, PR, L), bf16)
    pay, mine, other, sums, scal = call(
        step_kernel,
        (sds((NA, PR, L), bf16), half, half, sds((NA + NB, L), f32), sds((8, L), f32)),
        flops=unit * 256,
        scratch_shapes=[vm((MA, ROWS), bf16), vm((MA, COLS), bf16)],
    )(plan, xs, yg, cots, wu, wv)
    pay, send = call(
        join_kernel,
        (sds((NA, PR, L), bf16), half),
        grid=(1,),
        in_specs=[full(NZ, PR, L), full(2, NZ, PR, L), tail(NA, 16, 8)],
        out_specs=(tail(NA, 16, 8), full(NZ, PR, L)),
        input_output_aliases={2: 0},
    )(mine, pair(other), pay)
    got_s = exchange(pay, SA)
    tot_s, send = call(
        pass_kernel,
        (sds((PR, L), f32), half),
        grid=(1,),
        in_specs=[full(NA, PR, L), tail(NZ, 16, 8)],
        out_specs=(full(PR, L), tail(NZ, 16, 8)),
        input_output_aliases={1: 1},
    )(got_s, send)
    got_t = exchange(send, "z")
    return call(final_kernel, (sds((D, L), f32), sds((D, L), f32)))(
        tot_s, got_t, src_points, tgt_points, sums, scal
    )


def solution(mesh):
    grid = Mesh(mesh.devices.reshape(4, 2, 4, 8), ("x", "c", "y", "z"))
    in_specs = (
        P(None, ("x", "c", "y", "z")),
        P(None, ("y", "z", "x", "c")),
        P(("x", "c")),
        P(("y", "z")),
        P(("x", "c")),
        P(("y", "z")),
    )
    out_specs = (P(None, ("x", "c", "y", "z")), P(None, ("y", "z", "x", "c")))
    return jax.shard_map(body, mesh=grid, in_specs=in_specs, out_specs=out_specs, check_vma=False)
```

```python
import jax
import jax.numpy as jnp
import numpy as np
from jax import lax
from jax.experimental import pallas as pl
from jax.experimental.pallas import tpu as pltpu
from jax.sharding import Mesh, PartitionSpec as P

blur_scale = 0.25
ridge_shift = 0.5
D = 64
L = 128
KP = 80
SA = ("x", "y")
NA = 16
NB = 16
NZ = 8
ROWS = NA * L
COLS = NB * L
MA = 208
PR = 144
LOG2E = 1.4426950408889634
GAIN = 2.0 * LOG2E / (blur_scale * D)
SHIFT = 15.0 / GAIN
f32 = jnp.float32
bf16 = jnp.bfloat16
HI = lax.Precision.HIGHEST
VMEM = 24 * 1024 * 1024
WIDE = 60 * 1024 * 1024


def split3(v):
    hi = v.astype(bf16)
    rest = v - hi.astype(f32)
    mid = rest.astype(bf16)
    low = (rest - mid.astype(f32)).astype(bf16)
    return hi, mid, low


def join3(block, at):
    return (
        block[at : at + 1].astype(f32)
        + block[at + 1 : at + 2].astype(f32)
        + block[at + 2 : at + 3].astype(f32)
    )


def sds(shape, dtype):
    return jax.ShapeDtypeStruct(shape, dtype)


def call(kernel, out_shape, flops=0, limit=VMEM, **kw):
    cost = pl.CostEstimate(flops=flops, bytes_accessed=1 << 20, transcendentals=0)
    return pl.pallas_call(
        kernel,
        out_shape=out_shape,
        cost_estimate=cost,
        compiler_params=pltpu.CompilerParams(vmem_limit_bytes=limit),
        **kw,
    )


def rows16(rows):
    mark = lax.broadcasted_iota(jnp.int32, (16, L), 0)
    out = jnp.zeros((16, L), f32)
    for k, row in enumerate(rows):
        out = jnp.where(mark == k, jnp.broadcast_to(row, (16, L)), out)
    return out


def parts(v):
    return [t.astype(f32) for t in split3(v)]


def encode(points, dual, cot, first):
    one = [jnp.ones((1, L), f32)] * 3
    none = [jnp.zeros((1, L), f32)] * 3
    wide = points.astype(f32)
    norm = jnp.sum(wide * wide, axis=0, keepdims=True)
    bias = (D / 2.0) * dual - 0.5 * norm
    if first:
        bias = bias - SHIFT
    tail = parts(bias) + one + parts(cot) + none if first else one + parts(bias) + none + parts(cot)
    return jnp.concatenate([points, rows16(tail).astype(bf16)], axis=0)


def cot_of(block, first):
    return join3(block, 70 if first else 73)


def encode_kernel(src, tgt, src_dual, src_cot, tgt_dual, tgt_cot, own, out):
    at = lax.axis_index("y") * 8 + lax.axis_index("z")
    own[...] = encode(src[...], src_dual[pl.ds(at, 1), :], src_cot[pl.ds(at, 1), :], True)
    at = lax.axis_index("x") * 2 + lax.axis_index("c")
    one = encode(tgt[...], tgt_dual[pl.ds(at, 1), :], tgt_cot[pl.ds(at, 1), :], False)
    out[...] = jnp.broadcast_to(one[None], out.shape)


def tgt_slot(k):
    return (k % 2) * NZ + k // 2


def stack_kernel(a, b, c, d, out):
    for k, part in enumerate((a, b, c, d)):
        out[k] = part[...]


def sweep_kernel(g0, g1, g2, g3, yg, plan, xs, cots, wu_out, part_out, xt, ya, bub, bvb, row, col):
    mx = lax.axis_index("x")
    my = lax.axis_index("y")
    for m, g in enumerate((g0, g1, g2, g3)):
        for k in range(4):
            at = lax.rem(mx + 4 - k, 4) * 4 + lax.rem(my + 4 - m, 4)
            xs[pl.ds(at, 1)] = g[k][None]
    pad = jnp.zeros((L - KP, L), f32)
    row_id = lax.broadcasted_iota(jnp.int32, (L, L), 0)
    pick = jnp.where((row_id >= 70) & (row_id < 73), 1.0, 0.0).astype(bf16)
    for k in range(NA):
        sl = slice(k * L, (k + 1) * L)
        block = xs[k]
        turned = jnp.concatenate([block.astype(f32), pad], axis=0).T.astype(bf16)
        xt[sl, :] = turned
        bub[sl, :] = jnp.dot(turned, pick, preferred_element_type=f32)
        cots[k : k + 1, :] = cot_of(block, True)
        other = yg[tgt_slot(k)]
        ya[:, sl] = jnp.concatenate([other, pad.astype(bf16)], axis=0)
        c = cot_of(other, False)
        cots[NA + k : NA + k + 1, :] = c
        bvb[:, sl] = jnp.broadcast_to(c, (8, L))
    rb, wide = 512, 256
    for r in range(ROWS // rb):
        rows = slice(r * rb, (r + 1) * rb)
        bu = bub[rows, :].reshape(rb // 8, 8, L)
        for n in range(COLS // wide):
            dots = jnp.dot(xt[rows, :], ya[:, n * wide : (n + 1) * wide], preferred_element_type=f32)
            p = jnp.exp2(dots * GAIN)
            plan[rows, n * wide : (n + 1) * wide] = p.astype(bf16)
            acc = None if n == 0 else row[rows, :].reshape(rb // 8, 8, L)
            for m in range(wide // L):
                sl = slice(n * wide + m * L, n * wide + (m + 1) * L)
                mixed = p[:, m * L : (m + 1) * L].reshape(rb // 8, 8, L) * (bu + bvb[:, sl][None])
                acc = mixed if acc is None else acc + mixed
                down = jnp.sum(mixed, axis=0)
                col[:, sl] = down if r == 0 else col[:, sl] + down
            row[rows, :] = acc.reshape(rb, L)
    wu = jnp.concatenate(
        [jnp.sum(row[k * L : (k + 1) * L, :].T, axis=0, keepdims=True) for k in range(NA)], axis=0
    )
    wv = jnp.concatenate(
        [jnp.sum(col[:, k * L : (k + 1) * L], axis=0, keepdims=True) for k in range(NB)], axis=0
    )
    bu = cots[0:NA]
    bv = cots[NA : NA + NB]
    bw = jnp.sum(wu * bu + wv * bv)
    bb = jnp.sum(bu * bu) / NA + jnp.sum(bv * bv) / NB
    mark = lax.broadcasted_iota(jnp.int32, (8, L), 0)
    wu_out[...] = wu
    part_out[...] = jnp.concatenate([wv, jnp.where(mark == 0, bw, bb)], axis=0)


def mix_kernel(wu, parts, send, own):
    total = parts[0] + parts[1]
    own[...] = total[0:NB]
    whole = jnp.concatenate([wu[...], total[NB:]], axis=0)
    send[...] = jnp.broadcast_to(whole[None], send.shape)


def relay_kernel(got, own, send):
    total = got[0]
    for k in range(1, got.shape[0]):
        total = total + got[k]
    whole = jnp.concatenate([own[...], total], axis=0)
    send[...] = jnp.broadcast_to(whole[None], send.shape)


def stack_side(out, sl, block, c, r):
    pts = block[0:D]
    wide = pts.astype(f32)
    out[0:D, sl] = pts
    out[D : 2 * D, sl] = (wide * c).astype(bf16)
    out[2 * D : 3 * D, sl] = (wide * r).astype(bf16)
    out[3 * D : MA, sl] = rows16([jnp.ones((1, L), f32)] + parts(r)).astype(bf16)


def finish_side(piece, c, r):
    base = piece[0:D]
    mass = piece[3 * D : 3 * D + 1]
    pushed = piece[3 * D + 1 : 3 * D + 2] + piece[3 * D + 2 : 3 * D + 3] + piece[3 * D + 3 : 3 * D + 4]
    t_b = c * base + piece[D : 2 * D]
    t_r = r * base + piece[2 * D : 3 * D]
    return t_b, t_r, r * mass + pushed, pushed, mass


def step_kernel(plan, xs, yg, cots, wu_in, wv_in, pay, mine, other, sums, scal, ax, ay):
    wu = wu_in[0, 0:NA]
    for k in range(1, NA):
        wu = wu + wu_in[k, 0:NA]
    wv = wv_in[0]
    for k in range(1, NZ):
        wv = wv + wv_in[k]
    bw = wv[NB : NB + 1]
    bb = wv[NB + 1 : NB + 2]
    wv = wv[0:NB]
    alpha = bb / (bw + ridge_shift * bb)
    scal[0:1, :] = alpha
    scal[1:2, :] = bb
    scal[2:8, :] = jnp.zeros((6, L), f32)
    sums[0:NA] = wu
    sums[NA : NA + NB] = wv
    bu, bv = cots[0:NA], cots[NA : NA + NB]
    ru = bu - alpha * (wu + ridge_shift * bu)
    rv = bv - alpha * (wv + ridge_shift * bv)
    rr = jnp.full((1, L), jnp.sum(ru * ru) / NA + jnp.sum(rv * rv) / NB, f32)
    for k in range(NA):
        stack_side(ax, slice(k * L, (k + 1) * L), xs[k], bu[k : k + 1], ru[k : k + 1])
    for k in range(NB):
        stack_side(ay, slice(k * L, (k + 1) * L), yg[tgt_slot(k)], bv[k : k + 1], rv[k : k + 1])
    flip = lax.axis_index("c") == 0
    quad = jnp.zeros((1, L), f32)
    tails = []
    wide = 256
    for n in range(COLS // wide):
        part = jnp.dot(ax[...], plan[:, n * wide : (n + 1) * wide], preferred_element_type=f32)
        blocks = []
        for m in range(2):
            at = 2 * n + m
            r = rv[at : at + 1]
            t_b, t_r, s_r, pushed, _ = finish_side(part[:, m * L : (m + 1) * L], bv[at : at + 1], r)
            quad = quad + r * (s_r + pushed)
            blocks.append((t_b, t_r))
            tails.append(s_r)
        (b0, r0), (b1, r1) = blocks
        mine[n, 0:D] = jnp.where(flip, b0, b1).astype(bf16)
        mine[n, D : 2 * D] = jnp.where(flip, r0, r1).astype(bf16)
        other[n, 0:D] = jnp.where(flip, b1, b0).astype(bf16)
        other[n, D : 2 * D] = jnp.where(flip, r1, r0).astype(bf16)
    for n in range(ROWS // wide):
        part = lax.dot_general(
            ay[...], plan[n * wide : (n + 1) * wide, :], (((1,), (1,)), ((), ())), preferred_element_type=f32
        )
        for m in range(2):
            at = 2 * n + m
            r = ru[at : at + 1]
            t_b, t_r, s_r, _, mass = finish_side(part[:, m * L : (m + 1) * L], bu[at : at + 1], r)
            quad = quad + r * r * mass
            pay[at, 0:D] = t_b.astype(bf16)
            pay[at, D : 2 * D] = t_r.astype(bf16)
            pay[at, 2 * D : PR] = rows16(parts(s_r)).astype(bf16)
    quad = jnp.full((1, L), jnp.sum(quad), f32)
    extra = parts(quad) + parts(rr)
    for n in range(NZ):
        s0, s1 = tails[2 * n], tails[2 * n + 1]
        mine[n, 2 * D : PR] = rows16(parts(jnp.where(flip, s0, s1)) + extra).astype(bf16)
        other[n, 2 * D : PR] = rows16(parts(jnp.where(flip, s1, s0)) + extra).astype(bf16)


def join_kernel(mine, both, pay_in, pay, send):
    got = both.at[1 - lax.axis_index("c")]
    a = mine[0, 2 * D :].astype(f32)
    b = got[0, 2 * D :].astype(f32)
    quad = join3(a, 3) + join3(b, 3)
    rr = join3(a, 6) + join3(b, 6)
    mark = lax.broadcasted_iota(jnp.int32, (16, L), 0)
    extra = rows16([jnp.zeros((1, L), f32)] * 3 + parts(quad) + parts(rr))
    for k in range(NA):
        pay[k] = jnp.where(mark < 3, pay_in[k].astype(f32), extra).astype(bf16)
    for k in range(NZ):
        send[k, 0 : 2 * D] = (mine[k, 0 : 2 * D].astype(f32) + got[k, 0 : 2 * D].astype(f32)).astype(bf16)
        s = join3(mine[k, 2 * D :], 0) + join3(got[k, 2 * D :], 0)
        send[k, 2 * D : PR] = rows16(parts(s)).astype(bf16)


def pass_kernel(got, send_in, tot, send):
    total = got[0].astype(f32)
    for k in range(1, NA):
        total = total + got[k].astype(f32)
    tot[...] = total
    quad = join3(total, 131)
    rr = join3(total, 134)
    mark = lax.broadcasted_iota(jnp.int32, (16, L), 0)
    extra = rows16([jnp.zeros((1, L), f32)] * 3 + parts(quad) + parts(rr))
    for k in range(NZ):
        send[k] = jnp.where(mark < 3, send_in[k].astype(f32), extra).astype(bf16)


def final_kernel(tot_s, got, src_ref, tgt_ref, sums, scal, out_s, out_t):
    tot_t = got[0].astype(f32)
    for k in range(1, NZ):
        tot_t = tot_t + got[k].astype(f32)
    alpha = scal[0:1, :]
    bb = scal[1:2, :]
    rr = join3(tot_t, 134)
    quad = join3(tot_t, 131) + ridge_shift * rr
    ratio = rr / bb
    step = rr / (quad - ratio * rr / alpha)
    scale = 2.0 / (blur_scale * D)
    c_b = scale * (alpha + step * ratio)
    c_r = scale * step
    si = lax.axis_index("x") * 4 + lax.axis_index("y")
    ti = lax.axis_index("z") * 2 + lax.axis_index("c")

    def combine(points, tot, s_b, out):
        s = c_b * s_b + c_r * join3(tot, 128)
        out[...] = points[...].astype(f32) * s - (c_b * tot[0:D] + c_r * tot[D : 2 * D])

    combine(src_ref, tot_s[...], sums[pl.ds(si, 1), :], out_s)
    combine(tgt_ref, tot_t, sums[pl.ds(NA + ti, 1), :], out_t)


def exchange(v, axes):
    return lax.all_to_all(v, axes, 0, 0, tiled=True)


def shift(v, axis, n, k):
    return lax.ppermute(v, axis, [(i, (i + k) % n) for i in range(n)])


def pair(v):
    return lax.all_gather(v, "c", axis=0, tiled=False)


def body(src_points, tgt_points, src_dual, tgt_dual, src_cot, tgt_cot):
    whole = lambda v: v.reshape(-1, L)
    own, send = call(encode_kernel, (sds((KP, L), bf16), sds((NZ, KP, L), bf16)), limit=WIDE)(
        src_points,
        tgt_points,
        whole(src_dual),
        whole(src_cot),
        whole(tgt_dual),
        whole(tgt_cot),
    )
    g0 = call(stack_kernel, sds((4, KP, L), bf16), flops=10000000000)(
        own, *[shift(own, "x", 4, k) for k in (1, 2, 3)]
    )
    yg = pair(exchange(send, "z")).reshape(NB, KP, L)
    g1, g2, g3 = [shift(g0, "y", 4, k) for k in (1, 2, 3)]
    unit = ROWS * COLS * 2
    vm = pltpu.VMEM
    plan, xs, cots, wu, part = call(
        sweep_kernel,
        (
            sds((ROWS, COLS), bf16),
            sds((NA, KP, L), bf16),
            sds((NA + NB, L), f32),
            sds((NA, L), f32),
            sds((NB + 8, L), f32),
        ),
        flops=unit * 400,
        scratch_shapes=[
            vm((ROWS, L), bf16),
            vm((L, COLS), bf16),
            vm((ROWS, L), f32),
            vm((8, COLS), f32),
            vm((ROWS, L), f32),
            vm((8, COLS), f32),
        ],
    )(g0, g1, g2, g3, yg)

    def tail(n, rows, at):
        return pl.BlockSpec((n, rows, L), lambda i: (0, at, 0))

    def full(*shape):
        return pl.BlockSpec(shape, lambda i: (0,) * len(shape))

    send, wv = call(
        mix_kernel,
        (sds((NA, 24, L), f32), sds((NB, L), f32)),
        grid=(1,),
        in_specs=[full(NA, L), full(2, NB + 8, L)],
        out_specs=(full(NA, 24, L), full(NB, L)),
    )(wu, pair(part))
    wu = exchange(send, SA)
    send = call(
        relay_kernel,
        sds((NZ, 24, L), f32),
        grid=(1,),
        in_specs=[tail(NA, 8, 2), full(NB, L)],
        out_specs=full(NZ, 24, L),
    )(wu, wv)
    wv = exchange(send, "z")
    half = sds((NZ, PR, L), bf16)
    pay, mine, other, sums, scal = call(
        step_kernel,
        (sds((NA, PR, L), bf16), half, half, sds((NA + NB, L), f32), sds((8, L), f32)),
        flops=unit * 256,
        scratch_shapes=[vm((MA, ROWS), bf16), vm((MA, COLS), bf16)],
    )(plan, xs, yg, cots, wu, wv)
    pay, send = call(
        join_kernel,
        (sds((NA, PR, L), bf16), half),
        grid=(1,),
        in_specs=[full(NZ, PR, L), full(2, NZ, PR, L), tail(NA, 16, 8)],
        out_specs=(tail(NA, 16, 8), full(NZ, PR, L)),
        input_output_aliases={2: 0},
    )(mine, pair(other), pay)
    got_s = exchange(pay, SA)
    tot_s, send = call(
        pass_kernel,
        (sds((PR, L), f32), half),
        grid=(1,),
        in_specs=[full(NA, PR, L), tail(NZ, 16, 8)],
        out_specs=(full(PR, L), tail(NZ, 16, 8)),
        input_output_aliases={1: 1},
    )(got_s, send)
    got_t = exchange(send, "z")
    return call(final_kernel, (sds((D, L), f32), sds((D, L), f32)))(
        tot_s, got_t, src_points, tgt_points, sums, scal
    )


def solution(mesh):
    grid = Mesh(mesh.devices.reshape(4, 2, 4, 8), ("x", "c", "y", "z"))
    in_specs = (
        P(None, ("x", "c", "y", "z")),
        P(None, ("y", "z", "x", "c")),
        P(("x", "c")),
        P(("y", "z")),
        P(("x", "c")),
        P(("y", "z")),
    )
    out_specs = (P(None, ("x", "c", "y", "z")), P(None, ("y", "z", "x", "c")))
    return jax.shard_map(body, mesh=grid, in_specs=in_specs, out_specs=out_specs, check_vma=False)
```

```python
import jax
import jax.numpy as jnp
import numpy as np
from jax import lax
from jax.experimental import pallas as pl
from jax.experimental.pallas import tpu as pltpu
from jax.sharding import Mesh, PartitionSpec as P

blur_scale = 0.25
ridge_shift = 0.5
D = 64
L = 128
KP = 80
SA = ("x", "y")
NA = 16
NB = 16
NZ = 8
ROWS = NA * L
COLS = NB * L
MA = 208
PR = 144
LOG2E = 1.4426950408889634
GAIN = 2.0 * LOG2E / (blur_scale * D)
SHIFT = 15.0 / GAIN
f32 = jnp.float32
bf16 = jnp.bfloat16
HI = lax.Precision.HIGHEST
VMEM = 24 * 1024 * 1024
WIDE = 60 * 1024 * 1024


def split3(v):
    hi = v.astype(bf16)
    rest = v - hi.astype(f32)
    mid = rest.astype(bf16)
    low = (rest - mid.astype(f32)).astype(bf16)
    return hi, mid, low


def join3(block, at):
    return (
        block[at : at + 1].astype(f32)
        + block[at + 1 : at + 2].astype(f32)
        + block[at + 2 : at + 3].astype(f32)
    )


def sds(shape, dtype):
    return jax.ShapeDtypeStruct(shape, dtype)


def call(kernel, out_shape, flops=0, limit=VMEM, **kw):
    cost = pl.CostEstimate(flops=flops, bytes_accessed=1 << 20, transcendentals=0)
    return pl.pallas_call(
        kernel,
        out_shape=out_shape,
        cost_estimate=cost,
        compiler_params=pltpu.CompilerParams(vmem_limit_bytes=limit),
        **kw,
    )


def rows16(rows):
    mark = lax.broadcasted_iota(jnp.int32, (16, L), 0)
    out = jnp.zeros((16, L), f32)
    for k, row in enumerate(rows):
        out = jnp.where(mark == k, jnp.broadcast_to(row, (16, L)), out)
    return out


def parts(v):
    return [t.astype(f32) for t in split3(v)]


def encode(points, dual, cot, first):
    one = [jnp.ones((1, L), f32)] * 3
    none = [jnp.zeros((1, L), f32)] * 3
    wide = points.astype(f32)
    norm = jnp.sum(wide * wide, axis=0, keepdims=True)
    bias = (D / 2.0) * dual - 0.5 * norm
    if first:
        bias = bias - SHIFT
    tail = parts(bias) + one + parts(cot) + none if first else one + parts(bias) + none + parts(cot)
    return jnp.concatenate([points, rows16(tail).astype(bf16)], axis=0)


def cot_of(block, first):
    return join3(block, 70 if first else 73)


def encode_kernel(src, tgt, src_dual, src_cot, tgt_dual, tgt_cot, own, out):
    at = lax.axis_index("y") * 8 + lax.axis_index("z")
    own[...] = encode(src[...], src_dual[pl.ds(at, 1), :], src_cot[pl.ds(at, 1), :], True)
    at = lax.axis_index("x") * 2 + lax.axis_index("c")
    one = encode(tgt[...], tgt_dual[pl.ds(at, 1), :], tgt_cot[pl.ds(at, 1), :], False)
    out[...] = jnp.broadcast_to(one[None], out.shape)


def tgt_slot(k):
    return (k % 2) * NZ + k // 2


def stack_kernel(a, b, c, d, out):
    for k, part in enumerate((a, b, c, d)):
        out[k] = part[...]


def sweep_kernel(g0, g1, g2, g3, yg, plan, xs, cots, wu_out, part_out, xt, ya, bub, bvb, row, col):
    mx = lax.axis_index("x")
    my = lax.axis_index("y")
    for m, g in enumerate((g0, g1, g2, g3)):
        for k in range(4):
            at = lax.rem(mx + 4 - k, 4) * 4 + lax.rem(my + 4 - m, 4)
            xs[pl.ds(at, 1)] = g[k][None]
    pad = jnp.zeros((L - KP, L), f32)
    row_id = lax.broadcasted_iota(jnp.int32, (L, L), 0)
    pick = jnp.where((row_id >= 70) & (row_id < 73), 1.0, 0.0).astype(bf16)
    for k in range(NA):
        sl = slice(k * L, (k + 1) * L)
        block = xs[k]
        turned = jnp.concatenate([block.astype(f32), pad], axis=0).T.astype(bf16)
        xt[sl, :] = turned
        bub[sl, :] = jnp.dot(turned, pick, preferred_element_type=f32)
        cots[k : k + 1, :] = cot_of(block, True)
        other = yg[tgt_slot(k)]
        ya[:, sl] = jnp.concatenate([other, pad.astype(bf16)], axis=0)
        c = cot_of(other, False)
        cots[NA + k : NA + k + 1, :] = c
        bvb[:, sl] = jnp.broadcast_to(c, (8, L))
    rb, wide = 512, 256
    for r in range(ROWS // rb):
        rows = slice(r * rb, (r + 1) * rb)
        bu = bub[rows, :].reshape(rb // 8, 8, L)
        for n in range(COLS // wide):
            dots = jnp.dot(xt[rows, :], ya[:, n * wide : (n + 1) * wide], preferred_element_type=f32)
            p = jnp.exp2(dots * GAIN)
            plan[rows, n * wide : (n + 1) * wide] = p.astype(bf16)
            acc = None if n == 0 else row[rows, :].reshape(rb // 8, 8, L)
            for m in range(wide // L):
                sl = slice(n * wide + m * L, n * wide + (m + 1) * L)
                mixed = p[:, m * L : (m + 1) * L].reshape(rb // 8, 8, L) * (bu + bvb[:, sl][None])
                acc = mixed if acc is None else acc + mixed
                down = jnp.sum(mixed, axis=0)
                col[:, sl] = down if r == 0 else col[:, sl] + down
            row[rows, :] = acc.reshape(rb, L)
    wu = jnp.concatenate(
        [jnp.sum(row[k * L : (k + 1) * L, :].T, axis=0, keepdims=True) for k in range(NA)], axis=0
    )
    wv = jnp.concatenate(
        [jnp.sum(col[:, k * L : (k + 1) * L], axis=0, keepdims=True) for k in range(NB)], axis=0
    )
    bu = cots[0:NA]
    bv = cots[NA : NA + NB]
    bw = jnp.sum(wu * bu + wv * bv)
    bb = jnp.sum(bu * bu) / NA + jnp.sum(bv * bv) / NB
    mark = lax.broadcasted_iota(jnp.int32, (8, L), 0)
    wu_out[...] = wu
    part_out[...] = jnp.concatenate([wv, jnp.where(mark == 0, bw, bb)], axis=0)


def mix_kernel(wu, parts, send, own):
    total = parts[0] + parts[1]
    own[...] = total[0:NB]
    whole = jnp.concatenate([wu[...], total[NB:]], axis=0)
    send[...] = jnp.broadcast_to(whole[None], send.shape)


def relay_kernel(got, own, send):
    total = got[0]
    for k in range(1, got.shape[0]):
        total = total + got[k]
    whole = jnp.concatenate([own[...], total], axis=0)
    send[...] = jnp.broadcast_to(whole[None], send.shape)


def stack_side(out, sl, block, c, r):
    pts = block[0:D]
    wide = pts.astype(f32)
    out[0:D, sl] = pts
    out[D : 2 * D, sl] = (wide * c).astype(bf16)
    out[2 * D : 3 * D, sl] = (wide * r).astype(bf16)
    out[3 * D : MA, sl] = rows16([jnp.ones((1, L), f32)] + parts(r) + parts(r * r)).astype(bf16)


def finish_side(piece, c, r):
    base = piece[0:D]
    mass = piece[3 * D : 3 * D + 1]
    pushed = piece[3 * D + 1 : 3 * D + 2] + piece[3 * D + 2 : 3 * D + 3] + piece[3 * D + 3 : 3 * D + 4]
    t_b = c * base + piece[D : 2 * D]
    t_r = r * base + piece[2 * D : 3 * D]
    return t_b, t_r, r * mass + pushed, pushed


def left_kernel(plan, xs, cots, wu_in, wv_in, mine, other, sums, scal, ax):
    wu = wu_in[0, 0:NA]
    for k in range(1, NA):
        wu = wu + wu_in[k, 0:NA]
    wv = wv_in[0]
    for k in range(1, NZ):
        wv = wv + wv_in[k]
    bw = wv[NB : NB + 1]
    bb = wv[NB + 1 : NB + 2]
    wv = wv[0:NB]
    alpha = bb / (bw + ridge_shift * bb)
    scal[0:1, :] = alpha
    scal[1:2, :] = bb
    scal[2:8, :] = jnp.zeros((6, L), f32)
    sums[0:NA] = wu
    sums[NA : NA + NB] = wv
    bu, bv = cots[0:NA], cots[NA : NA + NB]
    ru = bu - alpha * (wu + ridge_shift * bu)
    rv = bv - alpha * (wv + ridge_shift * bv)
    rr = jnp.full((1, L), jnp.sum(ru * ru) / NA + jnp.sum(rv * rv) / NB, f32)
    for k in range(NA):
        stack_side(ax, slice(k * L, (k + 1) * L), xs[k], bu[k : k + 1], ru[k : k + 1])
    flip = lax.axis_index("c") == 0
    quad = jnp.zeros((1, L), f32)
    tails = []
    wide = 256
    for n in range(COLS // wide):
        part = jnp.dot(ax[...], plan[:, n * wide : (n + 1) * wide], preferred_element_type=f32)
        blocks = []
        for m in range(2):
            at = 2 * n + m
            r = rv[at : at + 1]
            piece = part[:, m * L : (m + 1) * L]
            t_b, t_r, s_r, pushed = finish_side(piece, bv[at : at + 1], r)
            quad = quad + r * (s_r + pushed)
            quad = quad + piece[3 * D + 4 : 3 * D + 5] + piece[3 * D + 5 : 3 * D + 6] + piece[3 * D + 6 : 3 * D + 7]
            blocks.append((t_b, t_r))
            tails.append(s_r)
        (b0, r0), (b1, r1) = blocks
        mine[n, 0:D] = jnp.where(flip, b0, b1).astype(bf16)
        mine[n, D : 2 * D] = jnp.where(flip, r0, r1).astype(bf16)
        other[n, 0:D] = jnp.where(flip, b1, b0).astype(bf16)
        other[n, D : 2 * D] = jnp.where(flip, r1, r0).astype(bf16)
    quad = jnp.full((1, L), jnp.sum(quad), f32)
    extra = parts(quad) + parts(rr)
    for n in range(NZ):
        s0, s1 = tails[2 * n], tails[2 * n + 1]
        mine[n, 2 * D : PR] = rows16(parts(jnp.where(flip, s0, s1)) + extra).astype(bf16)
        other[n, 2 * D : PR] = rows16(parts(jnp.where(flip, s1, s0)) + extra).astype(bf16)


def right_kernel(plan, yg, cots, sums, scal, pay, ay):
    alpha = scal[0:1, :]
    bu, bv = cots[0:NA], cots[NA : NA + NB]
    ru = bu - alpha * (sums[0:NA] + ridge_shift * bu)
    rv = bv - alpha * (sums[NA : NA + NB] + ridge_shift * bv)
    for k in range(NB):
        stack_side(ay, slice(k * L, (k + 1) * L), yg[tgt_slot(k)], bv[k : k + 1], rv[k : k + 1])
    wide = 256
    for n in range(ROWS // wide):
        part = lax.dot_general(
            ay[...], plan[n * wide : (n + 1) * wide, :], (((1,), (1,)), ((), ())), preferred_element_type=f32
        )
        for m in range(2):
            at = 2 * n + m
            t_b, t_r, s_r, _ = finish_side(part[:, m * L : (m + 1) * L], bu[at : at + 1], ru[at : at + 1])
            pay[at, 0:D] = t_b.astype(bf16)
            pay[at, D : 2 * D] = t_r.astype(bf16)
            pay[at, 2 * D : PR] = rows16(parts(s_r)).astype(bf16)


def join_kernel(mine, got, pay_in, pay, send):
    a = mine[0, 2 * D :].astype(f32)
    b = got[0, 2 * D :].astype(f32)
    quad = join3(a, 3) + join3(b, 3)
    rr = join3(a, 6) + join3(b, 6)
    mark = lax.broadcasted_iota(jnp.int32, (16, L), 0)
    extra = rows16([jnp.zeros((1, L), f32)] * 3 + parts(quad) + parts(rr))
    for k in range(NA):
        pay[k] = jnp.where(mark < 3, pay_in[k].astype(f32), extra).astype(bf16)
    for k in range(NZ):
        send[k, 0 : 2 * D] = (mine[k, 0 : 2 * D].astype(f32) + got[k, 0 : 2 * D].astype(f32)).astype(bf16)
        s = join3(mine[k, 2 * D :], 0) + join3(got[k, 2 * D :], 0)
        send[k, 2 * D : PR] = rows16(parts(s)).astype(bf16)


def pass_kernel(got, send_in, tot, send):
    total = got[0].astype(f32)
    for k in range(1, NA):
        total = total + got[k].astype(f32)
    tot[...] = total
    quad = join3(total, 131)
    rr = join3(total, 134)
    mark = lax.broadcasted_iota(jnp.int32, (16, L), 0)
    extra = rows16([jnp.zeros((1, L), f32)] * 3 + parts(quad) + parts(rr))
    for k in range(NZ):
        send[k] = jnp.where(mark < 3, send_in[k].astype(f32), extra).astype(bf16)


def final_kernel(tot_s, got, src_ref, tgt_ref, sums, scal, out_s, out_t):
    tot_t = got[0].astype(f32)
    for k in range(1, NZ):
        tot_t = tot_t + got[k].astype(f32)
    alpha = scal[0:1, :]
    bb = scal[1:2, :]
    rr = join3(tot_t, 134)
    quad = join3(tot_t, 131) + ridge_shift * rr
    ratio = rr / bb
    step = rr / (quad - ratio * rr / alpha)
    scale = 2.0 / (blur_scale * D)
    c_b = scale * (alpha + step * ratio)
    c_r = scale * step
    si = lax.axis_index("x") * 4 + lax.axis_index("y")
    ti = lax.axis_index("z") * 2 + lax.axis_index("c")

    def combine(points, tot, s_b, out):
        s = c_b * s_b + c_r * join3(tot, 128)
        out[...] = points[...].astype(f32) * s - (c_b * tot[0:D] + c_r * tot[D : 2 * D])

    combine(src_ref, tot_s[...], sums[pl.ds(si, 1), :], out_s)
    combine(tgt_ref, tot_t, sums[pl.ds(NA + ti, 1), :], out_t)


def exchange(v, axes):
    return lax.all_to_all(v, axes, 0, 0, tiled=True)


def shift(v, axis, n, k):
    return lax.ppermute(v, axis, [(i, (i + k) % n) for i in range(n)])


def pair(v):
    return lax.all_gather(v, "c", axis=0, tiled=False)


def body(src_points, tgt_points, src_dual, tgt_dual, src_cot, tgt_cot):
    whole = lambda v: v.reshape(-1, L)
    own, send = call(encode_kernel, (sds((KP, L), bf16), sds((NZ, KP, L), bf16)), limit=WIDE)(
        src_points,
        tgt_points,
        whole(src_dual),
        whole(src_cot),
        whole(tgt_dual),
        whole(tgt_cot),
    )
    g0 = call(stack_kernel, sds((4, KP, L), bf16), flops=10000000000)(
        own, *[shift(own, "x", 4, k) for k in (1, 2, 3)]
    )
    yg = pair(exchange(send, "z")).reshape(NB, KP, L)
    g1, g2, g3 = [shift(g0, "y", 4, k) for k in (1, 2, 3)]
    unit = ROWS * COLS * 2
    vm = pltpu.VMEM
    plan, xs, cots, wu, part = call(
        sweep_kernel,
        (
            sds((ROWS, COLS), bf16),
            sds((NA, KP, L), bf16),
            sds((NA + NB, L), f32),
            sds((NA, L), f32),
            sds((NB + 8, L), f32),
        ),
        flops=unit * 400,
        scratch_shapes=[
            vm((ROWS, L), bf16),
            vm((L, COLS), bf16),
            vm((ROWS, L), f32),
            vm((8, COLS), f32),
            vm((ROWS, L), f32),
            vm((8, COLS), f32),
        ],
    )(g0, g1, g2, g3, yg)

    def tail(n, rows, at):
        return pl.BlockSpec((n, rows, L), lambda i: (0, at, 0))

    def full(*shape):
        return pl.BlockSpec(shape, lambda i: (0,) * len(shape))

    send, wv = call(
        mix_kernel,
        (sds((NA, 24, L), f32), sds((NB, L), f32)),
        grid=(1,),
        in_specs=[full(NA, L), full(2, NB + 8, L)],
        out_specs=(full(NA, 24, L), full(NB, L)),
    )(wu, pair(part))
    wu = exchange(send, SA)
    send = call(
        relay_kernel,
        sds((NZ, 24, L), f32),
        grid=(1,),
        in_specs=[tail(NA, 8, 2), full(NB, L)],
        out_specs=full(NZ, 24, L),
    )(wu, wv)
    wv = exchange(send, "z")
    half = sds((NZ, PR, L), bf16)
    mine, other, sums, scal = call(
        left_kernel,
        (half, half, sds((NA + NB, L), f32), sds((8, L), f32)),
        flops=unit * 256,
        scratch_shapes=[vm((MA, ROWS), bf16)],
    )(plan, xs, cots, wu, wv)
    pay = call(
        right_kernel,
        sds((NA, PR, L), bf16),
        flops=unit * 256,
        scratch_shapes=[vm((MA, COLS), bf16)],
    )(plan, yg, cots, sums, scal)
    pay, send = call(
        join_kernel,
        (sds((NA, PR, L), bf16), half),
        grid=(1,),
        in_specs=[full(NZ, PR, L), full(NZ, PR, L), tail(NA, 16, 8)],
        out_specs=(tail(NA, 16, 8), full(NZ, PR, L)),
        input_output_aliases={2: 0},
    )(mine, shift(other, "c", 2, 1), pay)
    got_s = exchange(pay, SA)
    tot_s, send = call(
        pass_kernel,
        (sds((PR, L), f32), half),
        grid=(1,),
        in_specs=[full(NA, PR, L), tail(NZ, 16, 8)],
        out_specs=(full(PR, L), tail(NZ, 16, 8)),
        input_output_aliases={1: 1},
    )(got_s, send)
    got_t = exchange(send, "z")
    return call(final_kernel, (sds((D, L), f32), sds((D, L), f32)))(
        tot_s, got_t, src_points, tgt_points, sums, scal
    )


def solution(mesh):
    grid = Mesh(mesh.devices.reshape(4, 2, 4, 8), ("x", "c", "y", "z"))
    in_specs = (
        P(None, ("x", "c", "y", "z")),
        P(None, ("y", "z", "x", "c")),
        P(("x", "c")),
        P(("y", "z")),
        P(("x", "c")),
        P(("y", "z")),
    )
    out_specs = (P(None, ("x", "c", "y", "z")), P(None, ("y", "z", "x", "c")))
    return jax.shard_map(body, mesh=grid, in_specs=in_specs, out_specs=out_specs, check_vma=False)
```

```python
import jax
import jax.numpy as jnp
import numpy as np
from jax import lax
from jax.experimental import pallas as pl
from jax.experimental.pallas import tpu as pltpu
from jax.sharding import Mesh, PartitionSpec as P

blur_scale = 0.25
ridge_shift = 0.5
D = 64
L = 128
KP = 80
SA = ("x", "y")
NA = 16
NB = 16
NZ = 8
ROWS = NA * L
COLS = NB * L
MA = 208
PR = 144
LOG2E = 1.4426950408889634
GAIN = 2.0 * LOG2E / (blur_scale * D)
SHIFT = 15.0 / GAIN
f32 = jnp.float32
bf16 = jnp.bfloat16
HI = lax.Precision.HIGHEST
VMEM = 24 * 1024 * 1024
WIDE = 60 * 1024 * 1024


def split3(v):
    hi = v.astype(bf16)
    rest = v - hi.astype(f32)
    mid = rest.astype(bf16)
    low = (rest - mid.astype(f32)).astype(bf16)
    return hi, mid, low


def join3(block, at):
    return (
        block[at : at + 1].astype(f32)
        + block[at + 1 : at + 2].astype(f32)
        + block[at + 2 : at + 3].astype(f32)
    )


def sds(shape, dtype):
    return jax.ShapeDtypeStruct(shape, dtype)


def call(kernel, out_shape, flops=0, limit=VMEM, **kw):
    cost = pl.CostEstimate(flops=flops, bytes_accessed=1 << 20, transcendentals=0)
    return pl.pallas_call(
        kernel,
        out_shape=out_shape,
        cost_estimate=cost,
        compiler_params=pltpu.CompilerParams(vmem_limit_bytes=limit),
        **kw,
    )


def rows16(rows):
    mark = lax.broadcasted_iota(jnp.int32, (16, L), 0)
    out = jnp.zeros((16, L), f32)
    for k, row in enumerate(rows):
        out = jnp.where(mark == k, jnp.broadcast_to(row, (16, L)), out)
    return out


def parts(v):
    return [t.astype(f32) for t in split3(v)]


def encode(points, dual, cot, first):
    one = [jnp.ones((1, L), f32)] * 3
    none = [jnp.zeros((1, L), f32)] * 3
    wide = points.astype(f32)
    norm = jnp.sum(wide * wide, axis=0, keepdims=True)
    bias = (D / 2.0) * dual - 0.5 * norm
    if first:
        bias = bias - SHIFT
    tail = parts(bias) + one + parts(cot) + none if first else one + parts(bias) + none + parts(cot)
    return jnp.concatenate([points, rows16(tail).astype(bf16)], axis=0)


def cot_of(block, first):
    return join3(block, 70 if first else 73)


def encode_kernel(src, tgt, src_dual, src_cot, tgt_dual, tgt_cot, own, out):
    at = lax.axis_index("y") * 8 + lax.axis_index("z")
    own[...] = encode(src[...], src_dual[pl.ds(at, 1), :], src_cot[pl.ds(at, 1), :], True)
    at = lax.axis_index("x") * 2 + lax.axis_index("c")
    one = encode(tgt[...], tgt_dual[pl.ds(at, 1), :], tgt_cot[pl.ds(at, 1), :], False)
    out[...] = jnp.broadcast_to(one[None], out.shape)


def tgt_slot(k):
    return (k % 2) * NZ + k // 2


def stack_kernel(a, b, c, d, out):
    for k, part in enumerate((a, b, c, d)):
        out[k] = part[...]


def sweep_kernel(g0, g1, g2, g3, yg, plan, xs, cots, row, part_out, xt, ya, bub, bvb, col):
    mx = lax.axis_index("x")
    my = lax.axis_index("y")
    for m, g in enumerate((g0, g1, g2, g3)):
        for k in range(4):
            at = lax.rem(mx + 4 - k, 4) * 4 + lax.rem(my + 4 - m, 4)
            xs[pl.ds(at, 1)] = g[k][None]
    pad = jnp.zeros((L - KP, L), f32)
    row_id = lax.broadcasted_iota(jnp.int32, (L, L), 0)
    pick = jnp.where((row_id >= 70) & (row_id < 73), 1.0, 0.0).astype(bf16)
    for k in range(NA):
        sl = slice(k * L, (k + 1) * L)
        block = xs[k]
        turned = jnp.concatenate([block.astype(f32), pad], axis=0).T.astype(bf16)
        xt[sl, :] = turned
        bub[sl, :] = jnp.dot(turned, pick, preferred_element_type=f32)
        cots[k : k + 1, :] = cot_of(block, True)
        other = yg[tgt_slot(k)]
        ya[:, sl] = jnp.concatenate([other, pad.astype(bf16)], axis=0)
        c = cot_of(other, False)
        cots[NA + k : NA + k + 1, :] = c
        bvb[:, sl] = jnp.broadcast_to(c, (8, L))
    rb, wide = 512, 256
    for r in range(ROWS // rb):
        rows = slice(r * rb, (r + 1) * rb)
        bu = bub[rows, :].reshape(rb // 8, 8, L)
        for n in range(COLS // wide):
            dots = jnp.dot(xt[rows, :], ya[:, n * wide : (n + 1) * wide], preferred_element_type=f32)
            p = jnp.exp2(dots * GAIN)
            plan[rows, n * wide : (n + 1) * wide] = p.astype(bf16)
            acc = None if n == 0 else row[rows, :].reshape(rb // 8, 8, L)
            for m in range(wide // L):
                sl = slice(n * wide + m * L, n * wide + (m + 1) * L)
                mixed = p[:, m * L : (m + 1) * L].reshape(rb // 8, 8, L) * (bu + bvb[:, sl][None])
                acc = mixed if acc is None else acc + mixed
                down = jnp.sum(mixed, axis=0)
                col[:, sl] = down if r == 0 else col[:, sl] + down
            row[rows, :] = acc.reshape(rb, L)
    wv = jnp.concatenate(
        [jnp.sum(col[:, k * L : (k + 1) * L], axis=0, keepdims=True) for k in range(NB)], axis=0
    )
    bu = cots[0:NA]
    bv = cots[NA : NA + NB]
    bw = jnp.sum(wv * bv) + jnp.sum(row[...] * bub[...])
    bb = jnp.sum(bu * bu) / NA + jnp.sum(bv * bv) / NB
    mark = lax.broadcasted_iota(jnp.int32, (8, L), 0)
    part_out[...] = jnp.concatenate([wv, jnp.where(mark == 0, bw, bb)], axis=0)


def turn_kernel(row, wu):
    for k in range(NA):
        wu[k : k + 1, :] = jnp.sum(row[k * L : (k + 1) * L, :].T, axis=0, keepdims=True)


def mix_kernel(wu, part, sib, send, own):
    total = part[...] + sib[...]
    own[...] = total[0:NB]
    whole = jnp.concatenate([wu[...], total[NB:]], axis=0)
    send[...] = jnp.broadcast_to(whole[None], send.shape)


def relay_kernel(got, own, send):
    total = got[0]
    for k in range(1, got.shape[0]):
        total = total + got[k]
    whole = jnp.concatenate([own[...], total], axis=0)
    send[...] = jnp.broadcast_to(whole[None], send.shape)


def stack_side(out, sl, block, c, r):
    pts = block[0:D]
    wide = pts.astype(f32)
    out[0:D, sl] = pts
    out[D : 2 * D, sl] = (wide * c).astype(bf16)
    out[2 * D : 3 * D, sl] = (wide * r).astype(bf16)
    out[3 * D : MA, sl] = rows16([jnp.ones((1, L), f32)] + parts(r) + parts(r * r)).astype(bf16)


def finish_side(piece, c, r):
    base = piece[0:D]
    mass = piece[3 * D : 3 * D + 1]
    pushed = piece[3 * D + 1 : 3 * D + 2] + piece[3 * D + 2 : 3 * D + 3] + piece[3 * D + 3 : 3 * D + 4]
    t_b = c * base + piece[D : 2 * D]
    t_r = r * base + piece[2 * D : 3 * D]
    return t_b, t_r, r * mass + pushed, pushed


def left_kernel(plan, xs, cots, wu_in, wv_in, mine, other, sums, scal, ax):
    wu = wu_in[0, 0:NA]
    for k in range(1, NA):
        wu = wu + wu_in[k, 0:NA]
    wv = wv_in[0]
    for k in range(1, NZ):
        wv = wv + wv_in[k]
    bw = wv[NB : NB + 1]
    bb = wv[NB + 1 : NB + 2]
    wv = wv[0:NB]
    alpha = bb / (bw + ridge_shift * bb)
    scal[0:1, :] = alpha
    scal[1:2, :] = bb
    scal[2:8, :] = jnp.zeros((6, L), f32)
    sums[0:NA] = wu
    sums[NA : NA + NB] = wv
    bu, bv = cots[0:NA], cots[NA : NA + NB]
    ru = bu - alpha * (wu + ridge_shift * bu)
    rv = bv - alpha * (wv + ridge_shift * bv)
    rr = jnp.full((1, L), jnp.sum(ru * ru) / NA + jnp.sum(rv * rv) / NB, f32)
    for k in range(NA):
        stack_side(ax, slice(k * L, (k + 1) * L), xs[k], bu[k : k + 1], ru[k : k + 1])
    flip = lax.axis_index("c") == 0
    quad = jnp.zeros((1, L), f32)
    tails = []
    wide = 256
    for n in range(COLS // wide):
        part = jnp.dot(ax[...], plan[:, n * wide : (n + 1) * wide], preferred_element_type=f32)
        blocks = []
        for m in range(2):
            at = 2 * n + m
            r = rv[at : at + 1]
            piece = part[:, m * L : (m + 1) * L]
            t_b, t_r, s_r, pushed = finish_side(piece, bv[at : at + 1], r)
            quad = quad + r * (s_r + pushed)
            quad = quad + piece[3 * D + 4 : 3 * D + 5] + piece[3 * D + 5 : 3 * D + 6] + piece[3 * D + 6 : 3 * D + 7]
            blocks.append((t_b, t_r))
            tails.append(s_r)
        (b0, r0), (b1, r1) = blocks
        mine[n, 0:D] = jnp.where(flip, b0, b1).astype(bf16)
        mine[n, D : 2 * D] = jnp.where(flip, r0, r1).astype(bf16)
        other[n, 0:D] = jnp.where(flip, b1, b0).astype(bf16)
        other[n, D : 2 * D] = jnp.where(flip, r1, r0).astype(bf16)
    quad = jnp.full((1, L), jnp.sum(quad), f32)
    extra = parts(quad) + parts(rr)
    for n in range(NZ):
        s0, s1 = tails[2 * n], tails[2 * n + 1]
        mine[n, 2 * D : PR] = rows16(parts(jnp.where(flip, s0, s1)) + extra).astype(bf16)
        other[n, 2 * D : PR] = rows16(parts(jnp.where(flip, s1, s0)) + extra).astype(bf16)


def right_kernel(plan, yg, cots, sums, scal, pay, ay):
    alpha = scal[0:1, :]
    bu, bv = cots[0:NA], cots[NA : NA + NB]
    ru = bu - alpha * (sums[0:NA] + ridge_shift * bu)
    rv = bv - alpha * (sums[NA : NA + NB] + ridge_shift * bv)
    for k in range(NB):
        stack_side(ay, slice(k * L, (k + 1) * L), yg[tgt_slot(k)], bv[k : k + 1], rv[k : k + 1])
    wide = 256
    for n in range(ROWS // wide):
        part = lax.dot_general(
            ay[...], plan[n * wide : (n + 1) * wide, :], (((1,), (1,)), ((), ())), preferred_element_type=f32
        )
        for m in range(2):
            at = 2 * n + m
            t_b, t_r, s_r, _ = finish_side(part[:, m * L : (m + 1) * L], bu[at : at + 1], ru[at : at + 1])
            pay[at, 0:D] = t_b.astype(bf16)
            pay[at, D : 2 * D] = t_r.astype(bf16)
            pay[at, 2 * D : PR] = rows16(parts(s_r)).astype(bf16)


def join_kernel(mine, got, pay_in, pay, send):
    a = mine[0, 2 * D :].astype(f32)
    b = got[0, 2 * D :].astype(f32)
    quad = join3(a, 3) + join3(b, 3)
    rr = join3(a, 6) + join3(b, 6)
    mark = lax.broadcasted_iota(jnp.int32, (16, L), 0)
    extra = rows16([jnp.zeros((1, L), f32)] * 3 + parts(quad) + parts(rr))
    for k in range(NA):
        pay[k] = jnp.where(mark < 3, pay_in[k].astype(f32), extra).astype(bf16)
    for k in range(NZ):
        send[k, 0 : 2 * D] = (mine[k, 0 : 2 * D].astype(f32) + got[k, 0 : 2 * D].astype(f32)).astype(bf16)
        s = join3(mine[k, 2 * D :], 0) + join3(got[k, 2 * D :], 0)
        send[k, 2 * D : PR] = rows16(parts(s)).astype(bf16)


def pass_kernel(got, send_in, tot, send):
    total = got[0].astype(f32)
    for k in range(1, NA):
        total = total + got[k].astype(f32)
    tot[...] = total
    quad = join3(total, 131)
    rr = join3(total, 134)
    mark = lax.broadcasted_iota(jnp.int32, (16, L), 0)
    extra = rows16([jnp.zeros((1, L), f32)] * 3 + parts(quad) + parts(rr))
    for k in range(NZ):
        send[k] = jnp.where(mark < 3, send_in[k].astype(f32), extra).astype(bf16)


def final_kernel(tot_s, got, src_ref, tgt_ref, sums, scal, out_s, out_t):
    tot_t = got[0].astype(f32)
    for k in range(1, NZ):
        tot_t = tot_t + got[k].astype(f32)
    alpha = scal[0:1, :]
    bb = scal[1:2, :]
    rr = join3(tot_t, 134)
    quad = join3(tot_t, 131) + ridge_shift * rr
    ratio = rr / bb
    step = rr / (quad - ratio * rr / alpha)
    scale = 2.0 / (blur_scale * D)
    c_b = scale * (alpha + step * ratio)
    c_r = scale * step
    si = lax.axis_index("x") * 4 + lax.axis_index("y")
    ti = lax.axis_index("z") * 2 + lax.axis_index("c")

    def combine(points, tot, s_b, out):
        s = c_b * s_b + c_r * join3(tot, 128)
        out[...] = points[...].astype(f32) * s - (c_b * tot[0:D] + c_r * tot[D : 2 * D])

    combine(src_ref, tot_s[...], sums[pl.ds(si, 1), :], out_s)
    combine(tgt_ref, tot_t, sums[pl.ds(NA + ti, 1), :], out_t)


def exchange(v, axes):
    return lax.all_to_all(v, axes, 0, 0, tiled=True)


def shift(v, axis, n, k):
    return lax.ppermute(v, axis, [(i, (i + k) % n) for i in range(n)])


def pair(v):
    return lax.all_gather(v, "c", axis=0, tiled=False)


def body(src_points, tgt_points, src_dual, tgt_dual, src_cot, tgt_cot):
    whole = lambda v: v.reshape(-1, L)
    own, send = call(encode_kernel, (sds((KP, L), bf16), sds((NZ, KP, L), bf16)), limit=WIDE)(
        src_points,
        tgt_points,
        whole(src_dual),
        whole(src_cot),
        whole(tgt_dual),
        whole(tgt_cot),
    )
    g0 = call(stack_kernel, sds((4, KP, L), bf16), flops=10000000000)(
        own, *[shift(own, "x", 4, k) for k in (1, 2, 3)]
    )
    yg = pair(exchange(send, "z")).reshape(NB, KP, L)
    g1, g2, g3 = [shift(g0, "y", 4, k) for k in (1, 2, 3)]
    unit = ROWS * COLS * 2
    vm = pltpu.VMEM
    plan, xs, cots, row, part = call(
        sweep_kernel,
        (
            sds((ROWS, COLS), bf16),
            sds((NA, KP, L), bf16),
            sds((NA + NB, L), f32),
            sds((ROWS, L), f32),
            sds((NB + 8, L), f32),
        ),
        flops=unit * 400,
        scratch_shapes=[
            vm((ROWS, L), bf16),
            vm((L, COLS), bf16),
            vm((ROWS, L), f32),
            vm((8, COLS), f32),
            vm((8, COLS), f32),
        ],
    )(g0, g1, g2, g3, yg)
    wu = call(turn_kernel, sds((NA, L), f32), flops=unit * 200)(row)

    def tail(n, rows, at):
        return pl.BlockSpec((n, rows, L), lambda i: (0, at, 0))

    def full(*shape):
        return pl.BlockSpec(shape, lambda i: (0,) * len(shape))

    send, wv = call(
        mix_kernel,
        (sds((NA, 24, L), f32), sds((NB, L), f32)),
        grid=(1,),
        in_specs=[full(NA, L), full(NB + 8, L), full(NB + 8, L)],
        out_specs=(full(NA, 24, L), full(NB, L)),
    )(wu, part, shift(part, "c", 2, 1))
    wu = exchange(send, SA)
    send = call(
        relay_kernel,
        sds((NZ, 24, L), f32),
        grid=(1,),
        in_specs=[tail(NA, 8, 2), full(NB, L)],
        out_specs=full(NZ, 24, L),
    )(wu, wv)
    wv = exchange(send, "z")
    half = sds((NZ, PR, L), bf16)
    mine, other, sums, scal = call(
        left_kernel,
        (half, half, sds((NA + NB, L), f32), sds((8, L), f32)),
        flops=unit * 256,
        scratch_shapes=[vm((MA, ROWS), bf16)],
    )(plan, xs, cots, wu, wv)
    pay = call(
        right_kernel,
        sds((NA, PR, L), bf16),
        flops=unit * 256,
        scratch_shapes=[vm((MA, COLS), bf16)],
    )(plan, yg, cots, sums, scal)
    pay, send = call(
        join_kernel,
        (sds((NA, PR, L), bf16), half),
        grid=(1,),
        in_specs=[full(NZ, PR, L), full(NZ, PR, L), tail(NA, 16, 8)],
        out_specs=(tail(NA, 16, 8), full(NZ, PR, L)),
        input_output_aliases={2: 0},
    )(mine, shift(other, "c", 2, 1), pay)
    got_s = exchange(pay, SA)
    tot_s, send = call(
        pass_kernel,
        (sds((PR, L), f32), half),
        grid=(1,),
        in_specs=[full(NA, PR, L), tail(NZ, 16, 8)],
        out_specs=(full(PR, L), tail(NZ, 16, 8)),
        input_output_aliases={1: 1},
    )(got_s, send)
    got_t = exchange(send, "z")
    return call(final_kernel, (sds((D, L), f32), sds((D, L), f32)))(
        tot_s, got_t, src_points, tgt_points, sums, scal
    )


def solution(mesh):
    grid = Mesh(mesh.devices.reshape(4, 2, 4, 8), ("x", "c", "y", "z"))
    in_specs = (
        P(None, ("x", "c", "y", "z")),
        P(None, ("y", "z", "x", "c")),
        P(("x", "c")),
        P(("y", "z")),
        P(("x", "c")),
        P(("y", "z")),
    )
    out_specs = (P(None, ("x", "c", "y", "z")), P(None, ("y", "z", "x", "c")))
    return jax.shard_map(body, mesh=grid, in_specs=in_specs, out_specs=out_specs, check_vma=False)
```

```python
import jax
import jax.numpy as jnp
import numpy as np
from jax import lax
from jax.experimental import pallas as pl
from jax.experimental.pallas import tpu as pltpu
from jax.sharding import Mesh, PartitionSpec as P

blur_scale = 0.25
ridge_shift = 0.5
D = 64
L = 128
KP = 80
SA = ("x", "y")
NA = 16
NB = 16
NZ = 8
ROWS = NA * L
COLS = NB * L
MA = 208
PR = 144
LOG2E = 1.4426950408889634
GAIN = 2.0 * LOG2E / (blur_scale * D)
SHIFT = 15.0 / GAIN
f32 = jnp.float32
bf16 = jnp.bfloat16
HI = lax.Precision.HIGHEST
VMEM = 24 * 1024 * 1024
WIDE = 60 * 1024 * 1024


def split3(v):
    hi = v.astype(bf16)
    rest = v - hi.astype(f32)
    mid = rest.astype(bf16)
    low = (rest - mid.astype(f32)).astype(bf16)
    return hi, mid, low


def join3(block, at):
    return (
        block[at : at + 1].astype(f32)
        + block[at + 1 : at + 2].astype(f32)
        + block[at + 2 : at + 3].astype(f32)
    )


def sds(shape, dtype):
    return jax.ShapeDtypeStruct(shape, dtype)


def call(kernel, out_shape, flops=0, limit=VMEM, **kw):
    cost = pl.CostEstimate(flops=flops, bytes_accessed=1 << 20, transcendentals=0)
    return pl.pallas_call(
        kernel,
        out_shape=out_shape,
        cost_estimate=cost,
        compiler_params=pltpu.CompilerParams(vmem_limit_bytes=limit),
        **kw,
    )


def rows16(rows):
    mark = lax.broadcasted_iota(jnp.int32, (16, L), 0)
    out = jnp.zeros((16, L), f32)
    for k, row in enumerate(rows):
        out = jnp.where(mark == k, jnp.broadcast_to(row, (16, L)), out)
    return out


def parts(v):
    return [t.astype(f32) for t in split3(v)]


def encode(points, dual, cot, first):
    one = [jnp.ones((1, L), f32)] * 3
    none = [jnp.zeros((1, L), f32)] * 3
    wide = points.astype(f32)
    norm = jnp.sum(wide * wide, axis=0, keepdims=True)
    bias = (D / 2.0) * dual - 0.5 * norm
    if first:
        bias = bias - SHIFT
    tail = parts(bias) + one + parts(cot) + none if first else one + parts(bias) + none + parts(cot)
    return jnp.concatenate([points, rows16(tail).astype(bf16)], axis=0)


def cot_of(block, first):
    return join3(block, 70 if first else 73)


def encode_kernel(src, tgt, src_dual, src_cot, tgt_dual, tgt_cot, own, out):
    at = lax.axis_index("y") * 8 + lax.axis_index("z")
    own[...] = encode(src[...], src_dual[pl.ds(at, 1), :], src_cot[pl.ds(at, 1), :], True)
    at = lax.axis_index("x") * 2 + lax.axis_index("c")
    one = encode(tgt[...], tgt_dual[pl.ds(at, 1), :], tgt_cot[pl.ds(at, 1), :], False)
    out[...] = jnp.broadcast_to(one[None], out.shape)


def tgt_slot(k):
    return (k % 2) * NZ + k // 2


def stack_kernel(a, b, c, d, out):
    for k, part in enumerate((a, b, c, d)):
        out[k] = part[...]


def sweep_kernel(g0, g1, g2, g3, yg, plan, xs, cots, row, part_out, xt, ya, bub, bvb, col):
    mx = lax.axis_index("x")
    my = lax.axis_index("y")
    for m, g in enumerate((g0, g1, g2, g3)):
        for k in range(4):
            at = lax.rem(mx + 4 - k, 4) * 4 + lax.rem(my + 4 - m, 4)
            xs[pl.ds(at, 1)] = g[k][None]
    pad = jnp.zeros((L - KP, L), f32)
    row_id = lax.broadcasted_iota(jnp.int32, (L, L), 0)
    pick = jnp.where((row_id >= 70) & (row_id < 73), 1.0, 0.0).astype(bf16)
    for k in range(NA):
        sl = slice(k * L, (k + 1) * L)
        block = xs[k]
        turned = jnp.concatenate([block.astype(f32), pad], axis=0).T.astype(bf16)
        xt[sl, :] = turned
        bub[sl, :] = jnp.dot(turned, pick, preferred_element_type=f32)
        cots[k : k + 1, :] = cot_of(block, True)
        other = yg[tgt_slot(k)]
        ya[:, sl] = jnp.concatenate([other, pad.astype(bf16)], axis=0)
        c = cot_of(other, False)
        cots[NA + k : NA + k + 1, :] = c
        bvb[:, sl] = jnp.broadcast_to(c, (8, L))
    rb, wide = 512, 256
    for r in range(ROWS // rb):
        rows = slice(r * rb, (r + 1) * rb)
        bu = bub[rows, :].reshape(rb // 8, 8, L)
        for n in range(COLS // wide):
            dots = jnp.dot(xt[rows, :], ya[:, n * wide : (n + 1) * wide], preferred_element_type=f32)
            p = jnp.exp2(dots * GAIN)
            plan[rows, n * wide : (n + 1) * wide] = p.astype(bf16)
            acc = None if n == 0 else row[rows, :].reshape(rb // 8, 8, L)
            for m in range(wide // L):
                sl = slice(n * wide + m * L, n * wide + (m + 1) * L)
                mixed = p[:, m * L : (m + 1) * L].reshape(rb // 8, 8, L) * (bu + bvb[:, sl][None])
                acc = mixed if acc is None else acc + mixed
                down = jnp.sum(mixed, axis=0)
                col[:, sl] = down if r == 0 else col[:, sl] + down
            row[rows, :] = acc.reshape(rb, L)
    wv = jnp.concatenate(
        [jnp.sum(col[:, k * L : (k + 1) * L], axis=0, keepdims=True) for k in range(NB)], axis=0
    )
    bu = cots[0:NA]
    bv = cots[NA : NA + NB]
    bw = jnp.sum(wv * bv) + jnp.sum(row[...] * bub[...])
    bb = jnp.sum(bu * bu) / NA + jnp.sum(bv * bv) / NB
    mark = lax.broadcasted_iota(jnp.int32, (8, L), 0)
    part_out[...] = jnp.concatenate([wv, jnp.where(mark == 0, bw, bb)], axis=0)


def turn_kernel(row, xs, yg, cots, wu, xb, yb):
    for k in range(NA):
        sl = slice(k * L, (k + 1) * L)
        for out, block, c in (
            (xb, xs[k], cots[k : k + 1, :]),
            (yb, yg[tgt_slot(k)], cots[NA + k : NA + k + 1, :]),
        ):
            out[0:D, sl] = block[0:D]
            out[D : 2 * D, sl] = (block[0:D].astype(f32) * c).astype(bf16)
        wu[k : k + 1, :] = jnp.sum(row[k * L : (k + 1) * L, :].T, axis=0, keepdims=True)


def mix_kernel(wu, part, sib, send, own):
    total = part[...] + sib[...]
    own[...] = total[0:NB]
    whole = jnp.concatenate([wu[...], total[NB:]], axis=0)
    send[...] = jnp.broadcast_to(whole[None], send.shape)


def relay_kernel(got, own, send):
    total = got[0]
    for k in range(1, got.shape[0]):
        total = total + got[k]
    whole = jnp.concatenate([own[...], total], axis=0)
    send[...] = jnp.broadcast_to(whole[None], send.shape)


def stack_side(out, sl, block, r):
    pts = block[0:D]
    wide = pts.astype(f32)
    out[2 * D : 3 * D, sl] = (wide * r).astype(bf16)
    out[3 * D : MA, sl] = rows16([jnp.ones((1, L), f32)] + parts(r) + parts(r * r)).astype(bf16)


def finish_side(piece, c, r):
    base = piece[0:D]
    mass = piece[3 * D : 3 * D + 1]
    pushed = piece[3 * D + 1 : 3 * D + 2] + piece[3 * D + 2 : 3 * D + 3] + piece[3 * D + 3 : 3 * D + 4]
    t_b = c * base + piece[D : 2 * D]
    t_r = r * base + piece[2 * D : 3 * D]
    return t_b, t_r, r * mass + pushed, pushed


def left_kernel(plan, xs, xb, cots, wu_in, wv_in, mine, other, sums, scal, ax):
    ax[0 : 2 * D, :] = xb[...]
    wu = wu_in[0, 0:NA]
    for k in range(1, NA):
        wu = wu + wu_in[k, 0:NA]
    wv = wv_in[0]
    for k in range(1, NZ):
        wv = wv + wv_in[k]
    bw = wv[NB : NB + 1]
    bb = wv[NB + 1 : NB + 2]
    wv = wv[0:NB]
    alpha = bb / (bw + ridge_shift * bb)
    scal[0:1, :] = alpha
    scal[1:2, :] = bb
    scal[2:8, :] = jnp.zeros((6, L), f32)
    sums[0:NA] = wu
    sums[NA : NA + NB] = wv
    bu, bv = cots[0:NA], cots[NA : NA + NB]
    ru = bu - alpha * (wu + ridge_shift * bu)
    rv = bv - alpha * (wv + ridge_shift * bv)
    rr = jnp.full((1, L), jnp.sum(ru * ru) / NA + jnp.sum(rv * rv) / NB, f32)
    for k in range(NA):
        stack_side(ax, slice(k * L, (k + 1) * L), xs[k], ru[k : k + 1])
    flip = lax.axis_index("c") == 0
    quad = jnp.zeros((1, L), f32)
    tails = []
    wide = 256
    for n in range(COLS // wide):
        part = jnp.dot(ax[...], plan[:, n * wide : (n + 1) * wide], preferred_element_type=f32)
        blocks = []
        for m in range(2):
            at = 2 * n + m
            r = rv[at : at + 1]
            piece = part[:, m * L : (m + 1) * L]
            t_b, t_r, s_r, pushed = finish_side(piece, bv[at : at + 1], r)
            quad = quad + r * (s_r + pushed)
            quad = quad + piece[3 * D + 4 : 3 * D + 5] + piece[3 * D + 5 : 3 * D + 6] + piece[3 * D + 6 : 3 * D + 7]
            blocks.append((t_b, t_r))
            tails.append(s_r)
        (b0, r0), (b1, r1) = blocks
        mine[n, 0:D] = jnp.where(flip, b0, b1).astype(bf16)
        mine[n, D : 2 * D] = jnp.where(flip, r0, r1).astype(bf16)
        other[n, 0:D] = jnp.where(flip, b1, b0).astype(bf16)
        other[n, D : 2 * D] = jnp.where(flip, r1, r0).astype(bf16)
    quad = jnp.full((1, L), jnp.sum(quad), f32)
    extra = parts(quad) + parts(rr)
    for n in range(NZ):
        s0, s1 = tails[2 * n], tails[2 * n + 1]
        mine[n, 2 * D : PR] = rows16(parts(jnp.where(flip, s0, s1)) + extra).astype(bf16)
        other[n, 2 * D : PR] = rows16(parts(jnp.where(flip, s1, s0)) + extra).astype(bf16)


def right_kernel(plan, yg, yb, cots, sums, scal, pay, ay):
    ay[0 : 2 * D, :] = yb[...]
    alpha = scal[0:1, :]
    bu, bv = cots[0:NA], cots[NA : NA + NB]
    ru = bu - alpha * (sums[0:NA] + ridge_shift * bu)
    rv = bv - alpha * (sums[NA : NA + NB] + ridge_shift * bv)
    for k in range(NB):
        stack_side(ay, slice(k * L, (k + 1) * L), yg[tgt_slot(k)], rv[k : k + 1])
    wide = 256
    for n in range(ROWS // wide):
        part = lax.dot_general(
            ay[...], plan[n * wide : (n + 1) * wide, :], (((1,), (1,)), ((), ())), preferred_element_type=f32
        )
        for m in range(2):
            at = 2 * n + m
            t_b, t_r, s_r, _ = finish_side(part[:, m * L : (m + 1) * L], bu[at : at + 1], ru[at : at + 1])
            pay[at, 0:D] = t_b.astype(bf16)
            pay[at, D : 2 * D] = t_r.astype(bf16)
            pay[at, 2 * D : PR] = rows16(parts(s_r)).astype(bf16)


def join_kernel(mine, got, pay_in, pay, send):
    a = mine[0, 2 * D :].astype(f32)
    b = got[0, 2 * D :].astype(f32)
    quad = join3(a, 3) + join3(b, 3)
    rr = join3(a, 6) + join3(b, 6)
    mark = lax.broadcasted_iota(jnp.int32, (16, L), 0)
    extra = rows16([jnp.zeros((1, L), f32)] * 3 + parts(quad) + parts(rr))
    for k in range(NA):
        pay[k] = jnp.where(mark < 3, pay_in[k].astype(f32), extra).astype(bf16)
    for k in range(NZ):
        send[k, 0 : 2 * D] = (mine[k, 0 : 2 * D].astype(f32) + got[k, 0 : 2 * D].astype(f32)).astype(bf16)
        s = join3(mine[k, 2 * D :], 0) + join3(got[k, 2 * D :], 0)
        send[k, 2 * D : PR] = rows16(parts(s)).astype(bf16)


def pass_kernel(got, send_in, tot, send):
    total = got[0].astype(f32)
    for k in range(1, NA):
        total = total + got[k].astype(f32)
    tot[...] = total
    quad = join3(total, 131)
    rr = join3(total, 134)
    mark = lax.broadcasted_iota(jnp.int32, (16, L), 0)
    extra = rows16([jnp.zeros((1, L), f32)] * 3 + parts(quad) + parts(rr))
    for k in range(NZ):
        send[k] = jnp.where(mark < 3, send_in[k].astype(f32), extra).astype(bf16)


def final_kernel(tot_s, got, src_ref, tgt_ref, sums, scal, out_s, out_t):
    tot_t = got[0].astype(f32)
    for k in range(1, NZ):
        tot_t = tot_t + got[k].astype(f32)
    alpha = scal[0:1, :]
    bb = scal[1:2, :]
    rr = join3(tot_t, 134)
    quad = join3(tot_t, 131) + ridge_shift * rr
    ratio = rr / bb
    step = rr / (quad - ratio * rr / alpha)
    scale = 2.0 / (blur_scale * D)
    c_b = scale * (alpha + step * ratio)
    c_r = scale * step
    si = lax.axis_index("x") * 4 + lax.axis_index("y")
    ti = lax.axis_index("z") * 2 + lax.axis_index("c")

    def combine(points, tot, s_b, out):
        s = c_b * s_b + c_r * join3(tot, 128)
        out[...] = points[...].astype(f32) * s - (c_b * tot[0:D] + c_r * tot[D : 2 * D])

    combine(src_ref, tot_s[...], sums[pl.ds(si, 1), :], out_s)
    combine(tgt_ref, tot_t, sums[pl.ds(NA + ti, 1), :], out_t)


def exchange(v, axes):
    return lax.all_to_all(v, axes, 0, 0, tiled=True)


def shift(v, axis, n, k):
    return lax.ppermute(v, axis, [(i, (i + k) % n) for i in range(n)])


def pair(v):
    return lax.all_gather(v, "c", axis=0, tiled=False)


def body(src_points, tgt_points, src_dual, tgt_dual, src_cot, tgt_cot):
    whole = lambda v: v.reshape(-1, L)
    own, send = call(encode_kernel, (sds((KP, L), bf16), sds((NZ, KP, L), bf16)), limit=WIDE)(
        src_points,
        tgt_points,
        whole(src_dual),
        whole(src_cot),
        whole(tgt_dual),
        whole(tgt_cot),
    )
    g0 = call(stack_kernel, sds((4, KP, L), bf16), flops=10000000000)(
        own, *[shift(own, "x", 4, k) for k in (1, 2, 3)]
    )
    yg = pair(exchange(send, "z")).reshape(NB, KP, L)
    g1, g2, g3 = [shift(g0, "y", 4, k) for k in (1, 2, 3)]
    unit = ROWS * COLS * 2
    vm = pltpu.VMEM
    plan, xs, cots, row, part = call(
        sweep_kernel,
        (
            sds((ROWS, COLS), bf16),
            sds((NA, KP, L), bf16),
            sds((NA + NB, L), f32),
            sds((ROWS, L), f32),
            sds((NB + 8, L), f32),
        ),
        flops=unit * 400,
        scratch_shapes=[
            vm((ROWS, L), bf16),
            vm((L, COLS), bf16),
            vm((ROWS, L), f32),
            vm((8, COLS), f32),
            vm((8, COLS), f32),
        ],
    )(g0, g1, g2, g3, yg)
    wu, xb, yb = call(
        turn_kernel,
        (sds((NA, L), f32), sds((2 * D, ROWS), bf16), sds((2 * D, COLS), bf16)),
        flops=unit * 200,
    )(row, xs, yg, cots)

    def tail(n, rows, at):
        return pl.BlockSpec((n, rows, L), lambda i: (0, at, 0))

    def full(*shape):
        return pl.BlockSpec(shape, lambda i: (0,) * len(shape))

    send, wv = call(
        mix_kernel,
        (sds((NA, 24, L), f32), sds((NB, L), f32)),
        grid=(1,),
        in_specs=[full(NA, L), full(NB + 8, L), full(NB + 8, L)],
        out_specs=(full(NA, 24, L), full(NB, L)),
    )(wu, part, shift(part, "c", 2, 1))
    wu = exchange(send, SA)
    send = call(
        relay_kernel,
        sds((NZ, 24, L), f32),
        grid=(1,),
        in_specs=[tail(NA, 8, 2), full(NB, L)],
        out_specs=full(NZ, 24, L),
    )(wu, wv)
    wv = exchange(send, "z")
    half = sds((NZ, PR, L), bf16)
    mine, other, sums, scal = call(
        left_kernel,
        (half, half, sds((NA + NB, L), f32), sds((8, L), f32)),
        flops=unit * 256,
        scratch_shapes=[vm((MA, ROWS), bf16)],
    )(plan, xs, xb, cots, wu, wv)
    pay = call(
        right_kernel,
        sds((NA, PR, L), bf16),
        flops=unit * 256,
        scratch_shapes=[vm((MA, COLS), bf16)],
    )(plan, yg, yb, cots, sums, scal)
    pay, send = call(
        join_kernel,
        (sds((NA, PR, L), bf16), half),
        grid=(1,),
        in_specs=[full(NZ, PR, L), full(NZ, PR, L), tail(NA, 16, 8)],
        out_specs=(tail(NA, 16, 8), full(NZ, PR, L)),
        input_output_aliases={2: 0},
    )(mine, shift(other, "c", 2, 1), pay)
    got_s = exchange(pay, SA)
    tot_s, send = call(
        pass_kernel,
        (sds((PR, L), f32), half),
        grid=(1,),
        in_specs=[full(NA, PR, L), tail(NZ, 16, 8)],
        out_specs=(full(PR, L), tail(NZ, 16, 8)),
        input_output_aliases={1: 1},
    )(got_s, send)
    got_t = exchange(send, "z")
    return call(final_kernel, (sds((D, L), f32), sds((D, L), f32)))(
        tot_s, got_t, src_points, tgt_points, sums, scal
    )


def solution(mesh):
    grid = Mesh(mesh.devices.reshape(4, 2, 4, 8), ("x", "c", "y", "z"))
    in_specs = (
        P(None, ("x", "c", "y", "z")),
        P(None, ("y", "z", "x", "c")),
        P(("x", "c")),
        P(("y", "z")),
        P(("x", "c")),
        P(("y", "z")),
    )
    out_specs = (P(None, ("x", "c", "y", "z")), P(None, ("y", "z", "x", "c")))
    return jax.shard_map(body, mesh=grid, in_specs=in_specs, out_specs=out_specs, check_vma=False)
```
